512 devices in a mesh: dp: 16 (over y, core), expert: 32 (over z, x).
Axes of the slice: x: 4, y: 8, z: 8, core: 2. Of those that a mesh axis runs over, the one named last changes fastest.
Arguments:
- tokens: bfloat16 [65536, 2048], P(('dp', 'expert')), may hold values from -6 to 6
- output_gradient: bfloat16 [65536, 2048], P(('dp', 'expert')), may hold values from -6 to 6
- selected_expert_index: int32 [65536, 8], P(('dp', 'expert')), may hold values from 0 to 95, as said below
- routing_weight_rows: float32 [65536, 8], P(('dp', 'expert')), may hold values from 0.05 to 1
- fixed_gate_up_weight: bfloat16 [32, 2048, 2048], P('expert', 'dp'), may hold values from -0.125 to 0.125
- fixed_down_weight_flipped: bfloat16 [32, 2048, 1024], P('expert', 'dp'), may hold values from -0.1875 to 0.1875
- gate_up_adapter_narrow: bfloat16 [32, 2048, 128], P('expert'), may hold values from -0.125 to 0.125
- gate_up_adapter_widen: bfloat16 [32, 128, 1024], P('expert'), may hold values from -0.75 to 0.75
- down_adapter_narrow: bfloat16 [32, 1024, 64], P('expert'), may hold values from -0.1875 to 0.1875
- down_adapter_widen: bfloat16 [32, 64, 2048], P('expert'), may hold values from -0.75 to 0.75
Outputs:
- grad_in_a: float32 [32, 2048, 128], P('expert', 'dp')
- grad_in_b: float32 [32, 128, 1024], P('expert', 'dp')
- grad_down_a: float32 [32, 1024, 64], P('expert', 'dp')
- grad_down_b: float32 [32, 64, 2048], P('expert', 'dp')
The draws below stay inside these ranges and needn't reach their ends.
Inputs may be any that keep to these rules, and one draw needn't show every extreme that they name: `selected_expert_index`: within the 128 tokens of one device no expert is chosen more than 16 times, and some experts are chosen exactly 16 times; no token chooses an expert twice.
All inputs are finite; a program needn't handle non-finite values.
Results may differ from the reference program's by a relative error of at most 0.0059.
Values may be sent and summed in bfloat16 or wider, within the bound.
No kernel may reach another device: no remote copies, remote signals or barrier semaphores. Data moves between devices by JAX's collectives and lax.ppermute only.
A program may use at most 64 MiB of HBM per device.

```python
import math
import jax
import jax.numpy as jnp
from jax import lax

MODEL_FEATURES = 2048
HIDDEN_UNITS = 1024
ADAPTER_RANK = 64
ROUTED = 96
TOPK = 8
TOK_DEV = 128
CAP = 16
TRAINED_EXPERTS = 32
TOKENS = 65536
N_DP = 16
N_EXPERT = 32


def route_block(key):
    keys = jax.random.split(key, 3)
    half = CAP // 2
    quota = ROUTED // 3
    shift = jax.random.randint(keys[0], (quota,), 0, half + 1).astype(jnp.int32)
    counts = jnp.concatenate([jnp.full((quota,), CAP, jnp.int32), half + shift, half - shift])
    bounds = jnp.cumsum(counts).astype(jnp.int32)
    pairs = jnp.arange(TOPK * TOK_DEV, dtype=jnp.int32)
    ranked = jnp.sum((pairs[:, None] >= bounds[None, :]).astype(jnp.int32), axis=1).astype(jnp.int32)
    labels = jax.random.permutation(keys[1], ROUTED).astype(jnp.int32)
    chosen = labels[ranked].reshape(TOPK, TOK_DEV).T
    order = jax.random.permutation(keys[2], TOK_DEV)
    return chosen[order]


def draw_selected_expert_index(key, part):
    key = jax.random.fold_in(key, 11)
    keys = jax.random.split(key, N_DP * N_EXPERT)
    blocks = jax.vmap(route_block)(keys)
    return blocks.reshape(N_DP * N_EXPERT * TOK_DEV, TOPK).astype(jnp.int32)


def block_levels(rng, extent, shards, smallest, top_value):
    def one(position, parts):
        heights = jax.random.uniform(jax.random.fold_in(jax.random.fold_in(rng, 6), position), (parts,), jnp.float32, smallest / len(shards), top_value / len(shards))
        return jnp.repeat(jnp.exp(heights), extent[position] // parts).reshape((-1,) + (1,) * (len(extent) - position - 1))

    gain = one(*shards[0])
    for cut in shards[1:]:
        gain = gain * one(*cut)
    return gain


def bell_draw(own_key, extent, spread, reach, cuts=(), held_as=jnp.bfloat16):
    gain = block_levels(own_key, extent, cuts, -0.22, 0.18) if cuts else 1.0
    entries = jax.random.normal(own_key, extent, jnp.float32) * spread * gain
    return jnp.minimum(jnp.maximum(entries, -reach), reach).astype(held_as)


def setup_inputs(seed: int = 0) -> dict:
    streams_of = jax.random.split(jax.random.key(seed), 11)
    tokens = bell_draw(streams_of[0], (TOKENS, MODEL_FEATURES), 1.0, 6.0, ((0, 512),))
    output_gradient = bell_draw(streams_of[1], (TOKENS, MODEL_FEATURES), 1.0, 6.0, ((0, 512),))
    selected_expert_index = draw_selected_expert_index(jax.random.fold_in(streams_of[10], 71), 0)
    routing_weight_rows = jnp.clip(jnp.exp(math.log(1.0) - 2.9957323 * jax.random.uniform(streams_of[3], (TOKENS, TOPK), jnp.float32) ** block_levels(streams_of[3], (TOKENS, TOPK), ((0, 512),), -0.2, 0.2)), 0.05, 1.0)
    fixed_gate_up_weight = bell_draw(streams_of[4], (TRAINED_EXPERTS, MODEL_FEATURES, 2 * HIDDEN_UNITS), MODEL_FEATURES ** -0.5, 0.125, ((0, 32), (1, 16)))
    fixed_down_weight_flipped = bell_draw(streams_of[5], (TRAINED_EXPERTS, MODEL_FEATURES, HIDDEN_UNITS), HIDDEN_UNITS ** -0.5, 0.1875, ((0, 32), (1, 16)))
    gate_up_adapter_narrow = bell_draw(streams_of[6], (TRAINED_EXPERTS, MODEL_FEATURES, 2 * ADAPTER_RANK), MODEL_FEATURES ** -0.5, 0.125, ((0, 32),))
    gate_up_adapter_widen = bell_draw(streams_of[7], (TRAINED_EXPERTS, 2 * ADAPTER_RANK, HIDDEN_UNITS), ADAPTER_RANK ** -0.5, 0.75, ((0, 32),))
    down_adapter_narrow = bell_draw(streams_of[8], (TRAINED_EXPERTS, HIDDEN_UNITS, ADAPTER_RANK), HIDDEN_UNITS ** -0.5, 0.1875, ((0, 32),))
    down_adapter_widen = bell_draw(streams_of[9], (TRAINED_EXPERTS, ADAPTER_RANK, MODEL_FEATURES), ADAPTER_RANK ** -0.5, 0.75, ((0, 32),))
    return dict(tokens=tokens, output_gradient=output_gradient, selected_expert_index=selected_expert_index, routing_weight_rows=routing_weight_rows, fixed_gate_up_weight=fixed_gate_up_weight, fixed_down_weight_flipped=fixed_down_weight_flipped, gate_up_adapter_narrow=gate_up_adapter_narrow, gate_up_adapter_widen=gate_up_adapter_widen, down_adapter_narrow=down_adapter_narrow, down_adapter_widen=down_adapter_widen)


def slot_table(block_ids, experts, capacity):
    flat = block_ids.reshape(-1)
    onehot = (flat[:, None] == jnp.arange(experts, dtype=jnp.int32)[None, :]).astype(jnp.int32)
    before = jnp.cumsum(onehot, axis=0) - onehot
    slot_pos = lax.optimization_barrier(jnp.sum(before * onehot, axis=1)).astype(jnp.int32)
    dest = jnp.where(flat < experts, flat * capacity + slot_pos, -1).astype(jnp.int32)
    match = dest[:, None] == jnp.arange(experts * capacity, dtype=jnp.int32)[None, :]
    filled = jnp.any(match, axis=0)
    rows = jnp.arange(flat.shape[0], dtype=jnp.int32)
    source = lax.optimization_barrier(jnp.sum(jnp.where(match, rows[:, None], 0), axis=0)).astype(jnp.int32)
    return (source, filled)

def per_expert_gradients(expert_input_rows, output_cotangent_rows, w_in, w_down_t, input_adapter_lower, input_adapter_upper, down_adapter_lower, down_adapter_upper, routing_factor):
    adapter_rank_size = down_adapter_lower.shape[1]
    width = w_down_t.shape[1]
    base = jnp.dot(expert_input_rows, w_in, preferred_element_type=jnp.float32)
    low = jnp.dot(expert_input_rows, input_adapter_lower, preferred_element_type=jnp.float32).astype(jnp.bfloat16)
    gate = base[:, :width] + 0.5 * jnp.dot(low[:, :adapter_rank_size], input_adapter_upper[:adapter_rank_size], preferred_element_type=jnp.float32)
    up = base[:, width:] + 0.5 * jnp.dot(low[:, adapter_rank_size:], input_adapter_upper[adapter_rank_size:], preferred_element_type=jnp.float32)
    sig = jax.nn.sigmoid(gate)
    silu = gate * sig
    hidden = (silu * up).astype(jnp.bfloat16)
    hlow = jnp.dot(hidden, down_adapter_lower, preferred_element_type=jnp.float32).astype(jnp.bfloat16)
    zlow = jnp.dot(output_cotangent_rows, down_adapter_upper.T, preferred_element_type=jnp.float32).astype(jnp.bfloat16)
    dhid = jnp.dot(output_cotangent_rows, w_down_t, preferred_element_type=jnp.float32)
    dhid = dhid + 0.5 * jnp.dot(zlow, down_adapter_lower.T, preferred_element_type=jnp.float32)
    dgate = (dhid * up * sig * (1.0 + gate * (1.0 - sig))).astype(jnp.bfloat16)
    dup = (dhid * silu).astype(jnp.bfloat16)
    vlow = jnp.concatenate([jnp.dot(dgate, input_adapter_upper[:adapter_rank_size].T, preferred_element_type=jnp.float32), jnp.dot(dup, input_adapter_upper[adapter_rank_size:].T, preferred_element_type=jnp.float32)], axis=1).astype(jnp.bfloat16)
    grad_ia = routing_factor * jnp.dot(expert_input_rows.T, vlow, preferred_element_type=jnp.float32)
    grad_ib = routing_factor * jnp.concatenate([jnp.dot(low[:, :adapter_rank_size].T, dgate, preferred_element_type=jnp.float32), jnp.dot(low[:, adapter_rank_size:].T, dup, preferred_element_type=jnp.float32)], axis=0)
    grad_da = routing_factor * jnp.dot(hidden.T, zlow, preferred_element_type=jnp.float32)
    grad_db = routing_factor * jnp.dot(hlow.T, output_cotangent_rows, preferred_element_type=jnp.float32)
    return (grad_ia, grad_ib, grad_da, grad_db)

def reference(tokens, output_gradient, selected_expert_index, routing_weight_rows, fixed_gate_up_weight, fixed_down_weight_flipped, gate_up_adapter_narrow, gate_up_adapter_widen, down_adapter_narrow, down_adapter_widen):
    blocks = N_DP * N_EXPERT
    sources, filled = jax.vmap(lambda b: slot_table(b, TRAINED_EXPERTS, CAP))(selected_expert_index.reshape(blocks, TOK_DEV, TOPK))
    routing_factor = 0.5 / math.sqrt(TOKENS)
    offsets = (jnp.arange(blocks, dtype=jnp.int32) * TOK_DEV)[:, None]

    def one_expert(expert_number):
        src = lax.dynamic_slice_in_dim(sources, expert_number * CAP, CAP, 1)
        fil = lax.dynamic_slice_in_dim(filled, expert_number * CAP, CAP, 1)
        tok = offsets + src // TOPK
        pick = src % TOPK
        expert_input_rows = jnp.where(fil[..., None], tokens[tok], jnp.zeros((), jnp.bfloat16)).reshape(blocks * CAP, MODEL_FEATURES)
        weight = routing_weight_rows[tok, pick]
        output_cotangent_rows = (weight[..., None] * output_gradient[tok].astype(jnp.float32)).astype(jnp.bfloat16)
        output_cotangent_rows = jnp.where(fil[..., None], output_cotangent_rows, jnp.zeros((), jnp.bfloat16)).reshape(blocks * CAP, MODEL_FEATURES)
        return per_expert_gradients(expert_input_rows, output_cotangent_rows, fixed_gate_up_weight[expert_number], fixed_down_weight_flipped[expert_number], gate_up_adapter_narrow[expert_number], gate_up_adapter_widen[expert_number], down_adapter_narrow[expert_number], down_adapter_widen[expert_number], routing_factor)
    grad_ia, grad_ib, grad_da, grad_db = lax.map(one_expert, jnp.arange(TRAINED_EXPERTS, dtype=jnp.int32))
    return (grad_ia, grad_ib, grad_da, grad_db)
```

```python
import functools
import math

import jax
import jax.numpy as jnp
from jax import lax
from jax.experimental import pallas as pl
from jax.experimental.pallas import tpu as pltpu
from jax.sharding import PartitionSpec as P

F32 = jnp.float32
BF16 = jnp.bfloat16
LANES = 128


def dot_nt(a, b):
    return lax.dot_general(a, b, (((1,), (1,)), ((), ())), preferred_element_type=F32)


def dot_nn(a, b):
    return lax.dot_general(a, b, (((1,), (0,)), ((), ())), preferred_element_type=F32)


def slot_ranks(sel, experts):
    topk, toks = sel.shape
    ids = lax.broadcasted_iota(jnp.int32, (experts, toks), 0)
    chosen = jnp.zeros((experts, toks), F32)
    for k in range(topk):
        chosen += jnp.where(sel[k : k + 1, :] == ids, 1.0, 0.0)
    earlier = lax.broadcasted_iota(jnp.int32, (toks, toks), 0) < lax.broadcasted_iota(
        jnp.int32, (toks, toks), 1
    )
    before = dot_nn(chosen.astype(BF16), jnp.where(earlier, 1.0, 0.0).astype(BF16))
    return jnp.where(chosen > 0.0, before, -1.0)


def pack_x_kernel(cap, sel_ref, tok_ref, out_ref, rank_s):
    step = pl.program_id(0)

    @pl.when(step == 0)
    def _():
        rank_s[...] = slot_ranks(sel_ref[...], rank_s.shape[0])

    rank = rank_s[pl.ds(pl.multiple_of(step * 8, 8), 8), :]
    slot = lax.broadcasted_iota(jnp.int32, (cap, rank.shape[1]), 0).astype(F32)
    onehot = jnp.concatenate(
        [jnp.where(rank[e : e + 1, :] == slot, 1.0, 0.0) for e in range(8)], axis=0
    )
    out_ref[...] = dot_nn(onehot.astype(BF16), tok_ref[...]).astype(BF16)


def pack_y_kernel(cap, sel_ref, wgt_ref, tok_ref, out_ref, rank_s, wgt_s):
    step = pl.program_id(0)

    @pl.when(step == 0)
    def _():
        sel = sel_ref[...]
        rank_s[...] = slot_ranks(sel, rank_s.shape[0])
        ids = lax.broadcasted_iota(jnp.int32, rank_s.shape, 0)
        total = jnp.zeros(rank_s.shape, F32)
        for k in range(sel.shape[0]):
            total += jnp.where(sel[k : k + 1, :] == ids, wgt_ref[k : k + 1, :], 0.0)
        wgt_s[...] = total

    rows = pl.ds(pl.multiple_of(step * 8, 8), 8)
    rank = rank_s[rows, :]
    wgt = wgt_s[rows, :]
    slot = lax.broadcasted_iota(jnp.int32, (cap, rank.shape[1]), 0).astype(F32)
    taken = [rank[e : e + 1, :] == slot for e in range(8)]
    onehot = jnp.concatenate([jnp.where(m, 1.0, 0.0) for m in taken], axis=0)
    weight = jnp.concatenate(
        [
            jnp.sum(jnp.where(taken[e], wgt[e : e + 1, :], 0.0), axis=1, keepdims=True)
            for e in range(8)
        ],
        axis=0,
    )
    out_ref[...] = (weight * dot_nn(onehot.astype(BF16), tok_ref[...])).astype(BF16)


def pack_rows(sel_t, wgt_t, tok, experts, cap):
    toks, width = tok.shape
    topk = sel_t.shape[0]
    steps = experts // 8
    whole = lambda shape: pl.BlockSpec(shape, lambda i: (0, 0))
    ranks = pltpu.VMEM((experts, toks), F32)
    common = dict(
        grid=(steps,),
        out_shape=jax.ShapeDtypeStruct((experts * cap, width), BF16),
        out_specs=pl.BlockSpec((8 * cap, width), lambda i: (i, 0)),
        cost_estimate=pl.CostEstimate(
            flops=2 * experts * cap * toks * width,
            bytes_accessed=2 * width * (toks + experts * cap),
            transcendentals=0,
        ),
        compiler_params=pltpu.CompilerParams(vmem_limit_bytes=16 * 2**20),
    )
    if wgt_t is None:
        return pl.pallas_call(
            functools.partial(pack_x_kernel, cap),
            in_specs=[whole((topk, toks)), whole((toks, width))],
            scratch_shapes=[ranks],
            name="pack_x",
            **common,
        )(sel_t, tok)
    return pl.pallas_call(
        functools.partial(pack_y_kernel, cap),
        in_specs=[whole((topk, toks)), whole((topk, toks)), whole((toks, width))],
        scratch_shapes=[ranks, ranks],
        name="pack_y",
        **common,
    )(sel_t, wgt_t, tok)


def tail_kernel(
    core_ref,
    y_ref,
    wd_ref,
    dw_ref,
    dn_ref,
    g1_ref,
    g2_ref,
    hid_ref,
    hlow_t_ref,
    low_t_ref,
    win_ref,
    x_hbm,
    keep_ref,
    send_ref,
    x_s,
    zt_s,
    z_s,
    vt_s,
    inb_s,
    dna_s,
    db_s,
    x_sem,
):
    step = pl.program_id(0)
    steps = pl.num_programs(0)
    rank = zt_s.shape[0]
    fetch_x = pltpu.make_async_copy(x_hbm, x_s, x_sem)

    @pl.when(step == 0)
    def _():
        fetch_x.start()
        zt = dot_nt(dw_ref[...], y_ref[...])
        zt_s[...] = zt.astype(BF16)
        z_s[...] = zt.T.astype(BF16)
        db_s[...] = dot_nn(hlow_t_ref[...], y_ref[...])
        vt_s[...] = jnp.zeros_like(vt_s)

    dhid = dot_nn(y_ref[...], wd_ref[...]) + 0.5 * dot_nt(z_s[...], dn_ref[...])
    dgate = (dhid * g1_ref[...]).astype(BF16)
    dup = (dhid * g2_ref[...]).astype(BF16)
    vt_s[:rank, :] += dot_nt(win_ref[:rank, :], dgate)
    vt_s[rank:, :] += dot_nt(win_ref[rank:, :], dup)
    inb_s[step, :rank, :] = dot_nn(low_t_ref[:rank, :], dgate)
    inb_s[step, rank:, :] = dot_nn(low_t_ref[rank:, :], dup)
    dna_s[step] = dot_nn(zt_s[...], hid_ref[...])

    @pl.when(step == steps - 1)
    def _():
        fetch_x.wait()
        even = core_ref[0] == 0
        ina = dot_nn(vt_s[...].astype(BF16), x_s[...])
        cols = inb_s.shape[2] // LANES
        width = db_s.shape[1] // 2
        half = rank // 2
        left = lax.broadcasted_iota(jnp.int32, (half, LANES), 1) < LANES // 2
        upper = lax.broadcasted_iota(jnp.int32, (8, LANES), 0) < 4
        for t in range(keep_ref.shape[0]):
            d = dna_s[t // cols][:, (t % cols) * LANES : (t % cols + 1) * LANES]
            top, low = d[:half], d[half:]
            middle = (
                jnp.where(left, top, pltpu.roll(low, LANES // 2, 1)),
                jnp.where(left, pltpu.roll(top, LANES // 2, 1), low),
            )
            last = ([], [])
            for b in range(width // LANES):
                p = db_s[8 * t : 8 * t + 8, b * LANES : (b + 1) * LANES]
                q = db_s[8 * t : 8 * t + 8, width + b * LANES : width + (b + 1) * LANES]
                last[0].append(jnp.where(upper, p, pltpu.roll(q, 4, 0)))
                last[1].append(jnp.where(upper, pltpu.roll(p, 4, 0), q))
            both = []
            for c in range(2):
                j = 2 * t + c
                rows = [ina[:, j * LANES : (j + 1) * LANES]]
                for s in range(inb_s.shape[0]):
                    for b in range(cols):
                        rows.append(inb_s[s, 8 * j : 8 * j + 8, b * LANES : (b + 1) * LANES])
                both.append(jnp.concatenate(rows + [middle[c]] + last[c], axis=0))
            keep_ref[t] = jnp.where(even, both[0], both[1]).astype(BF16)
            send_ref[t] = jnp.where(even, both[1], both[0]).astype(BF16)


def tail(core, y, wd, dw, dn, g1, g2, hidden, hlow_t, low_t, win, x, parts):
    slots, width = y.shape
    units = wd.shape[1]
    rank = dw.shape[0]
    block = 256
    steps = units // block
    rows = (2 * rank * units + units * rank + rank * width) // (parts * LANES) + width // parts
    whole = lambda a: pl.BlockSpec(a.shape, lambda i: (0, 0))
    cols = lambda a: pl.BlockSpec((a.shape[0], block), lambda i: (0, i))
    out = jax.ShapeDtypeStruct((parts // 2, rows, LANES), BF16)
    out_spec = pl.BlockSpec(out.shape, lambda i: (0, 0, 0))
    return pl.pallas_call(
        tail_kernel,
        grid=(steps,),
        in_specs=[
            pl.BlockSpec(memory_space=pltpu.SMEM),
            whole(y),
            cols(wd),
            whole(dw),
            pl.BlockSpec((block, rank), lambda i: (i, 0)),
            cols(g1),
            cols(g2),
            cols(hidden),
            whole(hlow_t),
            whole(low_t),
            cols(win),
            pl.BlockSpec(memory_space=pl.ANY),
        ],
        out_shape=(out, out),
        out_specs=(out_spec, out_spec),
        scratch_shapes=[
            pltpu.VMEM((slots, width), BF16),
            pltpu.VMEM((rank, slots), BF16),
            pltpu.VMEM((slots, rank), BF16),
            pltpu.VMEM((2 * rank, slots), F32),
            pltpu.VMEM((steps, 2 * rank, block), F32),
            pltpu.VMEM((steps, rank, block), F32),
            pltpu.VMEM((rank, width), F32),
            pltpu.SemaphoreType.DMA,
        ],
        cost_estimate=pl.CostEstimate(
            flops=2 * slots * width * (units + 4 * rank),
            bytes_accessed=2 * width * (2 * slots + units) + 10 * slots * units,
            transcendentals=0,
        ),
        compiler_params=pltpu.CompilerParams(vmem_limit_bytes=40 * 2**20),
        name="gradients",
    )(core, y, wd, dw, dn, g1, g2, hidden, hlow_t, low_t, win, x)


def finish_kernel(factor, parts_ref, ina_ref, inb_ref, dna_ref, dnb_ref):
    total = parts_ref[0].astype(F32)
    for i in range(1, parts_ref.shape[0]):
        total += parts_ref[i].astype(F32)
    total *= factor
    width = ina_ref.shape[1]
    ina_ref[0] = total[:width].T
    at = width
    for b in range(inb_ref.shape[2] // LANES):
        inb_ref[0, :, b * LANES : (b + 1) * LANES] = total[at : at + 8]
        at += 8
    half = dna_ref.shape[2] // 2
    d = total[at : at + half]
    at += half
    both = jnp.concatenate([d, pltpu.roll(d, LANES // 2, 1)], axis=0)
    dna_ref[0] = both.T[: dna_ref.shape[1]]
    reach = dnb_ref.shape[2] // 2
    for b in range(reach // LANES):
        e = total[at : at + 8]
        at += 8
        dnb_ref[0, :, b * LANES : (b + 1) * LANES] = e[:4]
        dnb_ref[0, :, reach + b * LANES : reach + (b + 1) * LANES] = e[4:]


def finish(parts, factor, shapes):
    return pl.pallas_call(
        functools.partial(finish_kernel, factor),
        out_shape=tuple(jax.ShapeDtypeStruct(s, F32) for s in shapes),
        name="sum_parts",
    )(parts)


def body(
    tokens,
    output_gradient,
    selected_expert_index,
    routing_weight_rows,
    fixed_gate_up_weight,
    fixed_down_weight_flipped,
    gate_up_adapter_narrow,
    gate_up_adapter_widen,
    down_adapter_narrow,
    down_adapter_widen,
):
    experts = lax.axis_size("expert")
    groups = lax.axis_size("dp")
    tok_rows, model_width = tokens.shape
    cap = tok_rows // 8
    width = fixed_down_weight_flipped.shape[2]
    rank = down_adapter_narrow.shape[2]
    slots = experts * cap
    factor = 0.5 / math.sqrt(tok_rows * groups * experts)
    sel_t = selected_expert_index.T
    wgt_t = routing_weight_rows.T

    w_gate_up = lax.all_gather(fixed_gate_up_weight[0], "dp", axis=0, tiled=True)
    w_down = lax.all_gather(fixed_down_weight_flipped[0], "dp", axis=0, tiled=True)

    x_send = pack_rows(sel_t, None, tokens, experts, cap).reshape(experts, cap, model_width)
    x = lax.all_to_all(x_send, "expert", 0, 0, tiled=True)
    y_send = pack_rows(sel_t, wgt_t, output_gradient, experts, cap)
    y_send, x = lax.optimization_barrier((y_send, x))
    y = lax.all_to_all(
        y_send.reshape(experts, cap, model_width), "expert", 0, 0, tiled=True
    ).reshape(slots, model_width)
    x = x.reshape(slots, model_width)

    narrow = gate_up_adapter_narrow[0]
    widen = gate_up_adapter_widen[0]
    down_narrow = down_adapter_narrow[0]
    down_widen = down_adapter_widen[0]
    base = jnp.dot(x, w_gate_up, preferred_element_type=F32)
    low = jnp.dot(x, narrow, preferred_element_type=F32).astype(BF16)
    gate = base[:, :width] + 0.5 * jnp.dot(low[:, :rank], widen[:rank], preferred_element_type=F32)
    up = base[:, width:] + 0.5 * jnp.dot(low[:, rank:], widen[rank:], preferred_element_type=F32)
    sig = jax.nn.sigmoid(gate)
    silu = gate * sig
    hidden = (silu * up).astype(BF16)
    g_gate = up * sig * (1.0 + gate * (1.0 - sig))
    hlow_t = lax.dot_general(
        down_narrow, hidden, (((0,), (1,)), ((), ())), preferred_element_type=F32
    ).astype(BF16)

    core = (lax.axis_index("dp") % 2).astype(jnp.int32).reshape(1)
    keep, send = tail(
        core, y, w_down, down_widen, down_narrow, g_gate, silu, hidden, hlow_t, low.T, widen, x, groups
    )
    other = lax.ppermute(send, "dp", [(i, i ^ 1) for i in range(groups)])
    pair = (keep.astype(F32) + other.astype(F32)).astype(BF16)
    lines = [[2 * i + c for i in range(groups // 2)] for c in range(2)]
    parts = lax.all_to_all(pair, "dp", 0, 0, tiled=True, axis_index_groups=lines)
    shapes = (
        (1, model_width // groups, 2 * rank),
        (1, 2 * rank // groups, width),
        (1, width // groups, rank),
        (1, rank // groups, model_width),
    )
    return finish(parts, factor, shapes)


def solution(mesh):
    in_specs = (
        P(("dp", "expert"), None),
        P(("dp", "expert"), None),
        P(("dp", "expert"), None),
        P(("dp", "expert"), None),
        P("expert", "dp", None),
        P("expert", "dp", None),
        P("expert", None, None),
        P("expert", None, None),
        P("expert", None, None),
        P("expert", None, None),
    )
    out_specs = (
        P("expert", "dp", None),
        P("expert", "dp", None),
        P("expert", "dp", None),
        P("expert", "dp", None),
    )
    return jax.shard_map(body, mesh=mesh, in_specs=in_specs, out_specs=out_specs, check_vma=False)
```

```python
import functools
import math

import jax
import jax.numpy as jnp
from jax import lax
from jax.experimental import pallas as pl
from jax.experimental.pallas import tpu as pltpu
from jax.sharding import PartitionSpec as P

F32 = jnp.float32
BF16 = jnp.bfloat16
LANES = 128
VMEM = 58 * 2**20


def dot_nt(a, b):
    return lax.dot_general(a, b, (((1,), (1,)), ((), ())), preferred_element_type=F32)


def dot_nn(a, b):
    return lax.dot_general(a, b, (((1,), (0,)), ((), ())), preferred_element_type=F32)


def slot_ranks(sel, experts):
    topk, toks = sel.shape
    ids = lax.broadcasted_iota(jnp.int32, (experts, toks), 0)
    chosen = jnp.zeros((experts, toks), F32)
    for k in range(topk):
        chosen += jnp.where(sel[k : k + 1, :] == ids, 1.0, 0.0)
    earlier = lax.broadcasted_iota(jnp.int32, (toks, toks), 0) < lax.broadcasted_iota(
        jnp.int32, (toks, toks), 1
    )
    before = dot_nn(chosen.astype(BF16), jnp.where(earlier, 1.0, 0.0).astype(BF16))
    return jnp.where(chosen > 0.0, before, -1.0)


def pack_kernel(cap, sel_ref, wgt_ref, tok_ref, cot_ref, out_ref, rank_s, wgt_s):
    step = pl.program_id(0)
    group = out_ref.shape[0]
    width = out_ref.shape[2]

    @pl.when(step == 0)
    def _():
        sel = sel_ref[...]
        rank_s[...] = slot_ranks(sel, rank_s.shape[0])
        ids = lax.broadcasted_iota(jnp.int32, rank_s.shape, 0)
        total = jnp.zeros(rank_s.shape, F32)
        for k in range(sel.shape[0]):
            total += jnp.where(sel[k : k + 1, :] == ids, wgt_ref[k : k + 1, :], 0.0)
        wgt_s[...] = total

    rows = pl.ds(pl.multiple_of(step * group, group), group)
    rank = rank_s[rows, :]
    wgt = wgt_s[rows, :]
    slot = lax.broadcasted_iota(jnp.int32, (cap, rank.shape[1]), 0).astype(F32)
    taken = [rank[e : e + 1, :] == slot for e in range(group)]
    onehot = jnp.concatenate([jnp.where(m, 1.0, 0.0) for m in taken], axis=0).astype(BF16)
    weight = jnp.concatenate(
        [
            jnp.sum(jnp.where(taken[e], wgt[e : e + 1, :], 0.0), axis=1, keepdims=True)
            for e in range(group)
        ],
        axis=0,
    )
    x = dot_nn(onehot, tok_ref[...]).astype(BF16)
    y = (weight * dot_nn(onehot, cot_ref[...])).astype(BF16)
    out_ref[:, :cap, :] = x.reshape(group, cap, width)
    out_ref[:, cap:, :] = y.reshape(group, cap, width)


def pack_rows(sel_t, wgt_t, tok, cot, experts, cap):
    toks, width = tok.shape
    group = 8
    whole = lambda a: pl.BlockSpec(a.shape, lambda i: (0, 0))
    ranks = pltpu.VMEM((experts, toks), F32)
    return pl.pallas_call(
        functools.partial(pack_kernel, cap),
        grid=(experts // group,),
        in_specs=[whole(sel_t), whole(wgt_t), whole(tok), whole(cot)],
        out_shape=jax.ShapeDtypeStruct((experts, 2 * cap, width), BF16),
        out_specs=pl.BlockSpec((group, 2 * cap, width), lambda i: (i, 0, 0)),
        scratch_shapes=[ranks, ranks],
        cost_estimate=pl.CostEstimate(
            flops=4 * experts * cap * toks * width,
            bytes_accessed=4 * width * (toks + experts * cap),
            transcendentals=0,
        ),
        compiler_params=pltpu.CompilerParams(vmem_limit_bytes=VMEM),
        name="pack_rows",
    )(sel_t, wgt_t, tok, cot)


def gradients_kernel(
    core_ref,
    x_ref,
    wg_ref,
    wu_ref,
    wd_ref,
    narrow_ref,
    dw_ref,
    dnt_ref,
    win_ref,
    rows_hbm,
    keep_ref,
    send_ref,
    y_s,
    low_s,
    lowt_s,
    z_s,
    zt_s,
    vt_s,
    hlt_s,
    inb_s,
    dna_s,
    y_sem,
):
    step = pl.program_id(0)
    steps = pl.num_programs(0)
    rank = zt_s.shape[0]
    slots = low_s.shape[0]
    cap, width = x_ref.shape[1:]
    fetch_y = pltpu.make_async_copy(rows_hbm.at[:, pl.ds(cap, cap), :], y_s, y_sem)
    x = x_ref[...].reshape(slots, width)

    @pl.when(step == 0)
    def _():
        fetch_y.start()
        low = dot_nn(x, narrow_ref[...])
        low_s[...] = low.astype(BF16)
        lowt_s[...] = low.T.astype(BF16)
        vt_s[...] = jnp.zeros_like(vt_s)
        hlt_s[...] = jnp.zeros_like(hlt_s)

    win = win_ref[...]
    first = lax.broadcasted_iota(jnp.int32, win.shape, 0) < rank
    zero = jnp.zeros_like(win)
    low = low_s[...]
    gate = dot_nn(x, wg_ref[...]) + 0.5 * dot_nn(low, jnp.where(first, win, zero))
    up = dot_nn(x, wu_ref[...]) + 0.5 * dot_nn(low, jnp.where(first, zero, win))

    @pl.when(step == 0)
    def _():
        fetch_y.wait()
        z = dot_nt(y_s[...].reshape(slots, width), dw_ref[...])
        z_s[...] = z.astype(BF16)
        zt_s[...] = z.T.astype(BF16)

    dhid = dot_nn(y_s[...].reshape(slots, width), wd_ref[...])
    dhid += 0.5 * dot_nn(z_s[...], dnt_ref[...])
    sig = jax.nn.sigmoid(gate)
    silu = gate * sig
    hidden = (silu * up).astype(BF16)
    dgate = (dhid * up * sig * (1.0 + gate * (1.0 - sig))).astype(BF16)
    dup = (dhid * silu).astype(BF16)
    hlt_s[...] += dot_nt(dnt_ref[...], hidden)
    dna_s[step] = dot_nn(zt_s[...], hidden)
    vt_s[:rank, :] += dot_nt(win[:rank, :], dgate)
    vt_s[rank:, :] += dot_nt(win[rank:, :], dup)
    inb_s[step, :rank, :] = dot_nn(lowt_s[:rank, :], dgate)
    inb_s[step, rank:, :] = dot_nn(lowt_s[rank:, :], dup)

    @pl.when(step == steps - 1)
    def _():
        even = core_ref[0] == 0
        ina = dot_nn(vt_s[...].astype(BF16), x)
        dnb = dot_nn(hlt_s[...].astype(BF16), y_s[...].reshape(slots, width))
        cols = inb_s.shape[2] // LANES
        reach = width // 2
        half = rank // 2
        left = lax.broadcasted_iota(jnp.int32, (half, LANES), 1) < LANES // 2
        upper = lax.broadcasted_iota(jnp.int32, (8, LANES), 0) < 4
        for t in range(keep_ref.shape[0]):
            d = dna_s[t // cols][:, (t % cols) * LANES : (t % cols + 1) * LANES]
            top, low = d[:half], d[half:]
            middle = (
                jnp.where(left, top, pltpu.roll(low, LANES // 2, 1)),
                jnp.where(left, pltpu.roll(top, LANES // 2, 1), low),
            )
            last = ([], [])
            for b in range(reach // LANES):
                p = dnb[8 * t : 8 * t + 8, b * LANES : (b + 1) * LANES]
                q = dnb[8 * t : 8 * t + 8, reach + b * LANES : reach + (b + 1) * LANES]
                last[0].append(jnp.where(upper, p, pltpu.roll(q, 4, 0)))
                last[1].append(jnp.where(upper, pltpu.roll(p, 4, 0), q))
            both = []
            for c in range(2):
                j = 2 * t + c
                rows = [ina[:, j * LANES : (j + 1) * LANES]]
                for s in range(inb_s.shape[0]):
                    for b in range(cols):
                        rows.append(inb_s[s, 8 * j : 8 * j + 8, b * LANES : (b + 1) * LANES])
                both.append(jnp.concatenate(rows + [middle[c]] + last[c], axis=0))
            keep_ref[t] = jnp.where(even, both[0], both[1]).astype(BF16)
            send_ref[t] = jnp.where(even, both[1], both[0]).astype(BF16)


def gradients(core, rows, weights, narrow, win, dnt, dw, parts):
    sources, pair, width = rows.shape
    cap = pair // 2
    slots = sources * cap
    rank, units = dnt.shape
    block = 256
    steps = units // block
    lines = (2 * rank * units + units * rank + rank * width) // (parts * LANES) + width // parts
    whole = lambda a: pl.BlockSpec(a.shape, lambda i: (0, 0))
    cols = lambda a, at: pl.BlockSpec((a.shape[0], block), lambda i: (0, at * steps + i))
    out = jax.ShapeDtypeStruct((parts // 2, lines, LANES), BF16)
    out_spec = pl.BlockSpec(out.shape, lambda i: (0, 0, 0))
    return pl.pallas_call(
        gradients_kernel,
        grid=(steps,),
        in_specs=[
            pl.BlockSpec(memory_space=pltpu.SMEM),
            pl.BlockSpec((sources, cap, width), lambda i: (0, 0, 0)),
            cols(weights, 0),
            cols(weights, 1),
            cols(weights, 2),
            whole(narrow),
            whole(dw),
            cols(dnt, 0),
            cols(win, 0),
            pl.BlockSpec(memory_space=pl.ANY),
        ],
        out_shape=(out, out),
        out_specs=(out_spec, out_spec),
        scratch_shapes=[
            pltpu.VMEM((sources, cap, width), BF16),
            pltpu.VMEM((slots, 2 * rank), BF16),
            pltpu.VMEM((2 * rank, slots), BF16),
            pltpu.VMEM((slots, rank), BF16),
            pltpu.VMEM((rank, slots), BF16),
            pltpu.VMEM((2 * rank, slots), F32),
            pltpu.VMEM((rank, slots), F32),
            pltpu.VMEM((steps, 2 * rank, block), F32),
            pltpu.VMEM((steps, rank, block), F32),
            pltpu.SemaphoreType.DMA,
        ],
        cost_estimate=pl.CostEstimate(
            flops=2 * slots * width * (3 * units + 6 * rank),
            bytes_accessed=2 * width * (2 * slots + 3 * units),
            transcendentals=slots * units,
        ),
        compiler_params=pltpu.CompilerParams(vmem_limit_bytes=VMEM),
        name="gradients",
    )(core, rows, weights, weights, weights, narrow, dw, dnt, win, rows)


def finish_kernel(factor, parts_ref, ina_ref, inb_ref, dna_ref, dnb_ref):
    total = parts_ref[0].astype(F32)
    for i in range(1, parts_ref.shape[0]):
        total += parts_ref[i].astype(F32)
    total *= factor
    width = ina_ref.shape[1]
    ina_ref[0] = total[:width].T
    at = width
    for b in range(inb_ref.shape[2] // LANES):
        inb_ref[0, :, b * LANES : (b + 1) * LANES] = total[at : at + 8]
        at += 8
    half = dna_ref.shape[2] // 2
    d = total[at : at + half]
    at += half
    both = jnp.concatenate([d, pltpu.roll(d, LANES // 2, 1)], axis=0)
    dna_ref[0] = both.T[: dna_ref.shape[1]]
    reach = dnb_ref.shape[2] // 2
    for b in range(reach // LANES):
        e = total[at : at + 8]
        at += 8
        dnb_ref[0, :, b * LANES : (b + 1) * LANES] = e[:4]
        dnb_ref[0, :, reach + b * LANES : reach + (b + 1) * LANES] = e[4:]


def finish(parts, factor, shapes):
    return pl.pallas_call(
        functools.partial(finish_kernel, factor),
        out_shape=tuple(jax.ShapeDtypeStruct(s, F32) for s in shapes),
        name="sum_parts",
    )(parts)


def body(
    tokens,
    output_gradient,
    selected_expert_index,
    routing_weight_rows,
    fixed_gate_up_weight,
    fixed_down_weight_flipped,
    gate_up_adapter_narrow,
    gate_up_adapter_widen,
    down_adapter_narrow,
    down_adapter_widen,
):
    experts = lax.axis_size("expert")
    groups = lax.axis_size("dp")
    tok_rows, model_width = tokens.shape
    cap = tok_rows // 8
    width = fixed_down_weight_flipped.shape[2]
    rank = down_adapter_narrow.shape[2]
    factor = 0.5 / math.sqrt(tok_rows * groups * experts)
    weights = jnp.concatenate([fixed_gate_up_weight[0], fixed_down_weight_flipped[0]], axis=1)
    weights = lax.all_gather(weights, "dp", axis=0, tiled=True)
    rows = pack_rows(
        selected_expert_index.T, routing_weight_rows.T, tokens, output_gradient, experts, cap
    )
    rows = lax.all_to_all(rows, "expert", 0, 0, tiled=True)
    core = (lax.axis_index("dp") % 2).astype(jnp.int32).reshape(1)
    keep, send = gradients(
        core,
        rows,
        weights,
        gate_up_adapter_narrow[0],
        gate_up_adapter_widen[0],
        down_adapter_narrow[0].T,
        down_adapter_widen[0],
        groups,
    )
    other = lax.ppermute(send, "dp", [(i, i ^ 1) for i in range(groups)])
    pair = (keep.astype(F32) + other.astype(F32)).astype(BF16)
    lines = [[2 * i + c for i in range(groups // 2)] for c in range(2)]
    parts = lax.all_to_all(pair, "dp", 0, 0, tiled=True, axis_index_groups=lines)
    shapes = (
        (1, model_width // groups, 2 * rank),
        (1, 2 * rank // groups, width),
        (1, width // groups, rank),
        (1, rank // groups, model_width),
    )
    return finish(parts, factor, shapes)


def solution(mesh):
    in_specs = (
        P(("dp", "expert"), None),
        P(("dp", "expert"), None),
        P(("dp", "expert"), None),
        P(("dp", "expert"), None),
        P("expert", "dp", None),
        P("expert", "dp", None),
        P("expert", None, None),
        P("expert", None, None),
        P("expert", None, None),
        P("expert", None, None),
    )
    out_specs = (
        P("expert", "dp", None),
        P("expert", "dp", None),
        P("expert", "dp", None),
        P("expert", "dp", None),
    )
    return jax.shard_map(body, mesh=mesh, in_specs=in_specs, out_specs=out_specs, check_vma=False)
```

```python
import functools
import math

import jax
import jax.numpy as jnp
from jax import lax
from jax.experimental import pallas as pl
from jax.experimental.pallas import tpu as pltpu
from jax.sharding import PartitionSpec as P

F32 = jnp.float32
BF16 = jnp.bfloat16
LANES = 128
VMEM = 44 * 2**20


def in_hbm(*arrays):
    return [pltpu.with_memory_space_constraint(a, pltpu.HBM) for a in arrays]


def dot_nt(a, b):
    return lax.dot_general(a, b, (((1,), (1,)), ((), ())), preferred_element_type=F32)


def dot_nn(a, b):
    return lax.dot_general(a, b, (((1,), (0,)), ((), ())), preferred_element_type=F32)


def slot_ranks(sel, experts):
    topk, toks = sel.shape
    ids = lax.broadcasted_iota(jnp.int32, (experts, toks), 0)
    chosen = jnp.zeros((experts, toks), F32)
    for k in range(topk):
        chosen += jnp.where(sel[k : k + 1, :] == ids, 1.0, 0.0)
    earlier = lax.broadcasted_iota(jnp.int32, (toks, toks), 0) < lax.broadcasted_iota(
        jnp.int32, (toks, toks), 1
    )
    before = dot_nn(chosen.astype(BF16), jnp.where(earlier, 1.0, 0.0).astype(BF16))
    return jnp.where(chosen > 0.0, before, -1.0)


def pack_kernel(
    cap, sel_hbm, wgt_hbm, tok_hbm, cot_hbm, out_hbm, sel_s, wgt_s, tok_s, cot_s, out_s, hot_s, row_s, sems
):
    experts, _, width = out_s.shape
    cols = width // 4

    def fetch(src, dst, i):
        copy = pltpu.make_async_copy(src, dst, sems.at[i])
        copy.start()
        return copy

    first = [fetch(sel_hbm, sel_s, 0), fetch(wgt_hbm, wgt_s, 1)]
    tok_in = fetch(tok_hbm, tok_s, 2)
    cot_in = fetch(cot_hbm, cot_s, 3)
    for copy in first:
        copy.wait()
    sel = sel_s[...]
    rank = slot_ranks(sel, experts)
    ids = lax.broadcasted_iota(jnp.int32, rank.shape, 0)
    wgt = jnp.zeros(rank.shape, F32)
    for k in range(sel.shape[0]):
        wgt += jnp.where(sel[k : k + 1, :] == ids, wgt_s[k : k + 1, :], 0.0)
    slot = lax.broadcasted_iota(jnp.int32, (cap, rank.shape[1]), 0).astype(F32)
    for e in range(experts):
        taken = rank[e : e + 1, :] == slot
        rows = pl.ds(e * cap, cap)
        hot_s[rows, :] = jnp.where(taken, 1.0, 0.0).astype(BF16)
        weight = jnp.sum(jnp.where(taken, wgt[e : e + 1, :], 0.0), axis=1, keepdims=True)
        row_s[rows, :] = jnp.broadcast_to(weight, (cap, LANES))
    tok_in.wait()
    cot_in.wait()
    copies = []
    for i in range(width // cols):
        at = pl.ds(i * cols, cols)
        x = dot_nn(hot_s[...], tok_s[:, at]).astype(BF16)
        out_s[:, :cap, at] = x.reshape(experts, cap, cols)
        y = dot_nn(hot_s[...], cot_s[:, at])
        y = (jnp.concatenate([row_s[...]] * (cols // LANES), axis=1) * y).astype(BF16)
        out_s[:, cap:, at] = y.reshape(experts, cap, cols)
        copies.append(fetch(out_s.at[:, :, at], out_hbm.at[:, :, at], 4 + i))
    for copy in copies:
        copy.wait()


def pack_rows(sel_t, wgt_t, tok, cot, experts, cap):
    toks, width = tok.shape
    like = lambda a: pltpu.VMEM(a.shape, a.dtype)
    out = pltpu.HBM((experts, 2 * cap, width), BF16)
    return pl.pallas_call(
        functools.partial(pack_kernel, cap),
        in_specs=[pl.BlockSpec(memory_space=pltpu.HBM)] * 4,
        out_shape=out,
        out_specs=pl.BlockSpec(memory_space=pltpu.HBM),
        scratch_shapes=[
            like(sel_t),
            like(wgt_t),
            like(tok),
            like(cot),
            pltpu.VMEM(out.shape, BF16),
            pltpu.VMEM((experts * cap, toks), BF16),
            pltpu.VMEM((experts * cap, LANES), F32),
            pltpu.SemaphoreType.DMA((8,)),
        ],
        cost_estimate=pl.CostEstimate(
            flops=4 * experts * cap * toks * width,
            bytes_accessed=4 * width * (toks + experts * cap),
            transcendentals=0,
        ),
        compiler_params=pltpu.CompilerParams(vmem_limit_bytes=VMEM),
        name="pack_rows",
    )(*in_hbm(sel_t, wgt_t, tok, cot))


def gather_weights(shards):
    groups = lax.axis_size("dp")
    chips = groups // 2
    core = lax.axis_index("dp") % 2
    swap = lambda a: lax.ppermute(a, "dp", [(i, i ^ 1) for i in range(groups)])
    ring = lambda a, way: lax.ppermute(a, "dp", [(i, (i + 2 * way(i)) % groups) for i in range(groups)])
    up = down = jnp.concatenate(shards, axis=1)
    held = [up]
    for _ in range(1, chips // 2):
        up = ring(up, lambda i: 1)
        down = ring(down, lambda i: -1)
        held += [up, down]
    held.append(ring(jnp.where(core == 0, up, down), lambda i: 1 if i % 2 == 0 else -1))
    return held + [swap(a) for a in held]


def piece_rows(chips, lines, chip, core):
    starts = [chip]
    for hop in range(1, chips // 2):
        starts += [chip - hop, chip + hop]
    starts.append(chip + chips // 2)
    return [
        pl.multiple_of((2 * lax.rem(at + chips, chips) + part) * lines, lines)
        for part in (core, 1 - core)
        for at in starts
    ]


def gradients_kernel(
    block,
    chips,
    place_ref,
    rows_hbm,
    narrow_hbm,
    dw_hbm,
    dnt_hbm,
    win_hbm,
    *refs,
):
    pieces, refs = refs[: 2 * chips], refs[2 * chips :]
    keep_ref, send_ref, x_s, y_s, w_s, narrow_s, dw_s, dnt_s, win_s = refs[:9]
    hid_s, dgate_s, dup_s, inb_s, dna_s, dnb_s, ina_s, sems = refs[9:]
    sources, pair, width = rows_hbm.shape
    cap = pair // 2
    slots = sources * cap
    rank, units = dnt_s.shape
    deeper = x_s.shape[2]
    steps = units // block
    used = iter(range(sems.shape[0]))

    def fetch(src, dst):
        copy = pltpu.make_async_copy(src, dst, sems.at[next(used)])
        copy.start()
        return copy

    def columns(part, step):
        return pl.ds(part * units + step * block, block)

    firsts = piece_rows(chips, pieces[0].shape[0], place_ref[0], place_ref[1])
    cols_in = {}

    def fetch_columns(part, step):
        at = columns(part, step)
        cols_in[part, step] = [
            fetch(piece.at[:, at], w_s.at[pl.ds(first, piece.shape[0]), at])
            for piece, first in zip(pieces, firsts)
        ]

    def wait_columns(part, step):
        for copy in cols_in[part, step]:
            copy.wait()

    x_in = fetch(rows_hbm.at[:, pl.ds(0, cap), :], x_s.at[:, :, pl.ds(0, width)])
    narrow_in = fetch(narrow_hbm, narrow_s)
    fetch_columns(0, 0)
    win_in = fetch(win_hbm, win_s)
    fetch_columns(1, 0)
    y_in = fetch(rows_hbm.at[:, pl.ds(cap, cap), :], y_s.at[:, :, pl.ds(0, width)])
    dw_in = fetch(dw_hbm, dw_s)
    dnt_in = fetch(dnt_hbm, dnt_s)

    def times(rows_ref, part, step):
        return dot_nn(rows_ref[...].reshape(slots, deeper), w_s[:, columns(part, step)])

    for step in range(steps):
        at = pl.ds(step * block, block)
        if step == 0:
            x_in.wait()
            narrow_in.wait()
            x = x_s[:, :, :width].reshape(slots, width)
            low_f = dot_nn(x, narrow_s[...])
            low = low_f.astype(BF16)
            low_t = low_f.T.astype(BF16)
            x_s[:, :, width:] = low.reshape(sources, cap, 2 * rank)
            win_in.wait()
            win = (0.5 * win_s[...].astype(F32)).astype(BF16)
            zero = jnp.zeros((rank, units), BF16)
            w_s[width:, :units] = jnp.concatenate([win[:rank], zero], axis=0)
            w_s[width:, units : 2 * units] = jnp.concatenate([zero, win[rank:]], axis=0)
        wait_columns(0, step)
        fetch_columns(2, step)
        gate = times(x_s, 0, step)
        wait_columns(1, step)
        if step + 1 < steps:
            fetch_columns(0, step + 1)
        up = times(x_s, 1, step)
        if step == 0:
            y_in.wait()
            dw_in.wait()
            dnt_in.wait()
            y = y_s[:, :, :width].reshape(slots, width)
            z_f = dot_nt(y, dw_s[...])
            z = z_f.astype(BF16)
            z_t = z_f.T.astype(BF16)
            z = jnp.concatenate([z, jnp.zeros_like(z)], axis=1)
            y_s[:, :, width:] = z.reshape(sources, cap, 2 * rank)
            dnt = (0.5 * dnt_s[...].astype(F32)).astype(BF16)
            w_s[width:, 2 * units :] = jnp.concatenate([dnt, zero], axis=0)
        wait_columns(2, step)
        if step + 1 < steps:
            fetch_columns(1, step + 1)
        dhid = times(y_s, 2, step)
        sig = jax.nn.sigmoid(gate)
        silu = gate * sig
        hid_s[:, at] = (silu * up).astype(BF16)
        dgate_s[:, at] = (dhid * up * sig * (1.0 + gate * (1.0 - sig))).astype(BF16)
        dup_s[:, at] = (dhid * silu).astype(BF16)

    hlow_t = dot_nt(dnt_s[...], hid_s[...]).astype(BF16)
    vlow_t = jnp.concatenate(
        [dot_nt(win_s[:rank, :], dgate_s[...]), dot_nt(win_s[rank:, :], dup_s[...])], axis=0
    ).astype(BF16)
    dna_s[...] = dot_nn(z_t, hid_s[...])
    inb_s[:rank, :] = dot_nn(low_t[:rank, :], dgate_s[...])
    inb_s[rank:, :] = dot_nn(low_t[rank:, :], dup_s[...])
    dnb_s[...] = dot_nn(hlow_t, y_s[:, :, :width].reshape(slots, width))
    ina_s[...] = dot_nn(vlow_t, x_s[:, :, :width].reshape(slots, width))

    even = place_ref[1] == 0
    reach = width // 2
    half = rank // 2
    left = lax.broadcasted_iota(jnp.int32, (half, LANES), 1) < LANES // 2
    upper = lax.broadcasted_iota(jnp.int32, (8, LANES), 0) < 4
    for t in range(keep_ref.shape[0]):
        d = dna_s[:, t * LANES : (t + 1) * LANES]
        top, bottom = d[:half], d[half:]
        middle = (
            jnp.where(left, top, pltpu.roll(bottom, LANES // 2, 1)),
            jnp.where(left, pltpu.roll(top, LANES // 2, 1), bottom),
        )
        last = ([], [])
        for b in range(reach // LANES):
            p = dnb_s[8 * t : 8 * t + 8, b * LANES : (b + 1) * LANES]
            q = dnb_s[8 * t : 8 * t + 8, reach + b * LANES : reach + (b + 1) * LANES]
            last[0].append(jnp.where(upper, p, pltpu.roll(q, 4, 0)))
            last[1].append(jnp.where(upper, pltpu.roll(p, 4, 0), q))
        both = []
        for c in range(2):
            j = 2 * t + c
            lines = [ina_s[:, j * LANES : (j + 1) * LANES]]
            for b in range(units // LANES):
                lines.append(inb_s[8 * j : 8 * j + 8, b * LANES : (b + 1) * LANES])
            both.append(jnp.concatenate(lines + [middle[c]] + last[c], axis=0))
        keep_ref[t] = jnp.where(even, both[0], both[1]).astype(BF16)
        send_ref[t] = jnp.where(even, both[1], both[0]).astype(BF16)


def gradients(place, rows, pieces, narrow, win, dnt, dw, parts):
    sources, pair, width = rows.shape
    cap = pair // 2
    slots = sources * cap
    rank, units = dnt.shape
    block = 512
    lines = (2 * rank * units + units * rank + rank * width) // (parts * LANES) + width // parts
    out = pltpu.VMEM((parts // 2, lines, LANES), BF16)
    out_spec = pl.BlockSpec(memory_space=pltpu.VMEM)
    acts = pltpu.VMEM((sources, cap, width + 2 * rank), BF16)
    hidden = pltpu.VMEM((slots, units), BF16)
    like = lambda a: pltpu.VMEM(a.shape, a.dtype)
    return pl.pallas_call(
        functools.partial(gradients_kernel, block, parts // 2),
        in_specs=[pl.BlockSpec(memory_space=pltpu.SMEM)]
        + [pl.BlockSpec(memory_space=pltpu.HBM)] * 5
        + [pl.BlockSpec(memory_space=pl.ANY)] * len(pieces),
        out_shape=(out, out),
        out_specs=(out_spec, out_spec),
        scratch_shapes=[
            acts,
            acts,
            pltpu.VMEM((width + 2 * rank, 3 * units), BF16),
            like(narrow),
            like(dw),
            like(dnt),
            like(win),
            hidden,
            hidden,
            hidden,
            pltpu.VMEM((2 * rank, units), F32),
            pltpu.VMEM((rank, units), F32),
            pltpu.VMEM((rank, width), F32),
            pltpu.VMEM((2 * rank, width), F32),
            pltpu.SemaphoreType.DMA((6 + 3 * len(pieces) * (units // block),)),
        ],
        cost_estimate=pl.CostEstimate(
            flops=2 * slots * width * (3 * units + 6 * rank),
            bytes_accessed=2 * width * (2 * slots + 3 * units),
            transcendentals=slots * units,
        ),
        compiler_params=pltpu.CompilerParams(vmem_limit_bytes=VMEM),
        name="gradients",
    )(place, *in_hbm(rows, narrow, dw, dnt, win, *pieces))


def finish_kernel(factor, parts_ref, ina_ref, inb_ref, dna_ref, dnb_ref):
    total = parts_ref[0].astype(F32)
    for i in range(1, parts_ref.shape[0]):
        total += parts_ref[i].astype(F32)
    total *= factor
    width = ina_ref.shape[1]
    ina_ref[0] = total[:width].T
    at = width
    for b in range(inb_ref.shape[2] // LANES):
        inb_ref[0, :, b * LANES : (b + 1) * LANES] = total[at : at + 8]
        at += 8
    half = dna_ref.shape[2] // 2
    d = total[at : at + half]
    at += half
    both = jnp.concatenate([d, pltpu.roll(d, LANES // 2, 1)], axis=0)
    dna_ref[0] = both.T[: dna_ref.shape[1]]
    reach = dnb_ref.shape[2] // 2
    for b in range(reach // LANES):
        e = total[at : at + 8]
        at += 8
        dnb_ref[0, :, b * LANES : (b + 1) * LANES] = e[:4]
        dnb_ref[0, :, reach + b * LANES : reach + (b + 1) * LANES] = e[4:]


def finish(parts, factor, shapes):
    return pl.pallas_call(
        functools.partial(finish_kernel, factor),
        out_shape=tuple(jax.ShapeDtypeStruct(s, F32) for s in shapes),
        name="sum_parts",
    )(parts)


def body(
    tokens,
    output_gradient,
    selected_expert_index,
    routing_weight_rows,
    fixed_gate_up_weight,
    fixed_down_weight_flipped,
    gate_up_adapter_narrow,
    gate_up_adapter_widen,
    down_adapter_narrow,
    down_adapter_widen,
):
    experts = lax.axis_size("expert")
    groups = lax.axis_size("dp")
    tok_rows, model_width = tokens.shape
    cap = tok_rows // 8
    width = fixed_down_weight_flipped.shape[2]
    rank = down_adapter_narrow.shape[2]
    factor = 0.5 / math.sqrt(tok_rows * groups * experts)
    pieces = gather_weights([fixed_gate_up_weight[0], fixed_down_weight_flipped[0]])
    rows = pack_rows(
        selected_expert_index.T, routing_weight_rows.T, tokens, output_gradient, experts, cap
    )
    rows = lax.all_to_all(rows, "expert", 0, 0, tiled=True)
    index = lax.axis_index("dp").astype(jnp.int32)
    place = jnp.stack([index // 2, index % 2])
    keep, send = gradients(
        place,
        rows,
        pieces,
        gate_up_adapter_narrow[0],
        gate_up_adapter_widen[0],
        down_adapter_narrow[0].T,
        down_adapter_widen[0],
        groups,
    )
    other = lax.ppermute(send, "dp", [(i, i ^ 1) for i in range(groups)])
    pair = (keep.astype(F32) + other.astype(F32)).astype(BF16)
    lines = [[2 * i + c for i in range(groups // 2)] for c in range(2)]
    parts = lax.all_to_all(pair, "dp", 0, 0, tiled=True, axis_index_groups=lines)
    shapes = (
        (1, model_width // groups, 2 * rank),
        (1, 2 * rank // groups, width),
        (1, width // groups, rank),
        (1, rank // groups, model_width),
    )
    return finish(parts, factor, shapes)


def solution(mesh):
    in_specs = (
        P(("dp", "expert"), None),
        P(("dp", "expert"), None),
        P(("dp", "expert"), None),
        P(("dp", "expert"), None),
        P("expert", "dp", None),
        P("expert", "dp", None),
        P("expert", None, None),
        P("expert", None, None),
        P("expert", None, None),
        P("expert", None, None),
    )
    out_specs = (
        P("expert", "dp", None),
        P("expert", "dp", None),
        P("expert", "dp", None),
        P("expert", "dp", None),
    )
    return jax.shard_map(body, mesh=mesh, in_specs=in_specs, out_specs=out_specs, check_vma=False)
```

```python
import functools
import math

import jax
import jax.numpy as jnp
from jax import lax
from jax.experimental import pallas as pl
from jax.experimental.pallas import tpu as pltpu
from jax.sharding import PartitionSpec as P

F32 = jnp.float32
BF16 = jnp.bfloat16
LANES = 128
BLOCK = 512
VMEM = 44 * 2**20


def in_hbm(*arrays):
    return [pltpu.with_memory_space_constraint(a, pltpu.HBM) for a in arrays]


def in_vmem(*arrays):
    return [pltpu.with_memory_space_constraint(a, pltpu.VMEM) for a in arrays]


def dot_nt(a, b):
    return lax.dot_general(a, b, (((1,), (1,)), ((), ())), preferred_element_type=F32)


def dot_nn(a, b):
    return lax.dot_general(a, b, (((1,), (0,)), ((), ())), preferred_element_type=F32)


def slot_ranks(sel, experts):
    topk, toks = sel.shape
    ids = lax.broadcasted_iota(jnp.int32, (experts, toks), 0)
    chosen = jnp.zeros((experts, toks), F32)
    for k in range(topk):
        chosen += jnp.where(sel[k : k + 1, :] == ids, 1.0, 0.0)
    earlier = lax.broadcasted_iota(jnp.int32, (toks, toks), 0) < lax.broadcasted_iota(
        jnp.int32, (toks, toks), 1
    )
    before = dot_nn(chosen.astype(BF16), jnp.where(earlier, 1.0, 0.0).astype(BF16))
    return jnp.where(chosen > 0.0, before, -1.0)


def pack_kernel(
    cap, sel_hbm, wgt_hbm, tok_hbm, cot_hbm, out_hbm, sel_s, wgt_s, tok_s, cot_s, out_s, hot_s, row_s, sems
):
    experts, _, width = out_s.shape
    cols = width // 8

    def fetch(src, dst, i):
        copy = pltpu.make_async_copy(src, dst, sems.at[i])
        copy.start()
        return copy

    first = [fetch(sel_hbm, sel_s, 0), fetch(wgt_hbm, wgt_s, 1)]
    tok_in = fetch(tok_hbm, tok_s, 2)
    cot_in = fetch(cot_hbm, cot_s, 3)
    for copy in first:
        copy.wait()
    sel = sel_s[...]
    rank = slot_ranks(sel, experts)
    ids = lax.broadcasted_iota(jnp.int32, rank.shape, 0)
    wgt = jnp.zeros(rank.shape, F32)
    for k in range(sel.shape[0]):
        wgt += jnp.where(sel[k : k + 1, :] == ids, wgt_s[k : k + 1, :], 0.0)
    slot = lax.broadcasted_iota(jnp.int32, (cap, rank.shape[1]), 0).astype(F32)
    for e in range(experts):
        taken = rank[e : e + 1, :] == slot
        rows = pl.ds(e * cap, cap)
        hot_s[rows, :] = jnp.where(taken, 1.0, 0.0).astype(BF16)
        weight = jnp.sum(jnp.where(taken, wgt[e : e + 1, :], 0.0), axis=1, keepdims=True)
        row_s[rows, :] = jnp.broadcast_to(weight, (cap, LANES))
    tok_in.wait()
    cot_in.wait()
    copies = []
    for i in range(width // cols):
        at = pl.ds(i * cols, cols)
        x = dot_nn(hot_s[...], tok_s[:, at]).astype(BF16)
        out_s[:, :cap, at] = x.reshape(experts, cap, cols)
        y = dot_nn(hot_s[...], cot_s[:, at])
        y = (jnp.concatenate([row_s[...]] * (cols // LANES), axis=1) * y).astype(BF16)
        out_s[:, cap:, at] = y.reshape(experts, cap, cols)
        copies.append(fetch(out_s.at[:, :, at], out_hbm.at[:, :, at], 4 + i))
    for copy in copies:
        copy.wait()


def pack_rows(sel_t, wgt_t, tok, cot, experts, cap):
    toks, width = tok.shape
    like = lambda a: pltpu.VMEM(a.shape, a.dtype)
    out = pltpu.HBM((experts, 2 * cap, width), BF16)
    return pl.pallas_call(
        functools.partial(pack_kernel, cap),
        in_specs=[pl.BlockSpec(memory_space=pltpu.HBM)] * 4,
        out_shape=out,
        out_specs=pl.BlockSpec(memory_space=pltpu.HBM),
        scratch_shapes=[
            like(sel_t),
            like(wgt_t),
            like(tok),
            like(cot),
            pltpu.VMEM(out.shape, BF16),
            pltpu.VMEM((experts * cap, toks), BF16),
            pltpu.VMEM((experts * cap, LANES), F32),
            pltpu.SemaphoreType.DMA((12,)),
        ],
        cost_estimate=pl.CostEstimate(
            flops=4 * experts * cap * toks * width,
            bytes_accessed=4 * width * (toks + experts * cap),
            transcendentals=0,
        ),
        compiler_params=pltpu.CompilerParams(vmem_limit_bytes=VMEM),
        name="pack_rows",
    )(*in_hbm(sel_t, wgt_t, tok, cot))


def column_blocks(gate_up, down):
    units = down.shape[1]
    cut = lambda a, first: a[:, first : first + BLOCK]
    blocks = []
    for at in range(0, units, BLOCK):
        blocks += [cut(gate_up, at), cut(gate_up, units + at), cut(down, at)]
    return blocks


def gather_weights(shards):
    groups = lax.axis_size("dp")
    chips = groups // 2
    core = lax.axis_index("dp") % 2
    swap = lambda a: lax.ppermute(a, "dp", [(i, i ^ 1) for i in range(groups)])
    ring = lambda a, way: lax.ppermute(a, "dp", [(i, (i + 2 * way(i)) % groups) for i in range(groups)])
    up = down = jnp.concatenate(shards, axis=1)
    held = [up]
    for _ in range(1, chips // 2):
        up = ring(up, lambda i: 1)
        down = ring(down, lambda i: -1)
        held += [up, down]
    held.append(ring(jnp.where(core == 0, up, down), lambda i: 1 if i % 2 == 0 else -1))
    return held + [swap(a) for a in held]


def piece_rows(chips, lines, chip, core):
    starts = [chip]
    for hop in range(1, chips // 2):
        starts += [chip - hop, chip + hop]
    starts.append(chip + chips // 2)
    return [
        pl.multiple_of((2 * lax.rem(at + chips, chips) + part) * lines, lines)
        for part in (core, 1 - core)
        for at in starts
    ]


def gradients_kernel(
    chips,
    place_ref,
    rows_hbm,
    narrow_s,
    dw_s,
    dnt_s,
    win_s,
    *refs,
):
    pieces, refs = refs[: 2 * chips], refs[2 * chips :]
    keep_ref, send_ref, x_rows, y_rows, x_s, y_s, w_s = refs[:7]
    hid_s, dgate_s, dup_s, inb_s, dna_s, dnb_s, ina_s, sems = refs[7:]
    slots = x_rows.shape[0]
    cap, width = x_s.shape[1:]
    rank, units = dnt_s.shape
    steps = units // BLOCK
    firsts = piece_rows(chips, pieces[0].shape[0], place_ref[0], place_ref[1])
    used = iter(range(sems.shape[0]))

    def fetch(src, dst):
        copy = pltpu.make_async_copy(src, dst, sems.at[next(used)])
        copy.start()
        return copy

    def fetch_blocks(first, last):
        at = pl.ds(first * BLOCK, (last - first) * BLOCK)
        return [
            fetch(piece.at[:, at], w_s.at[pl.ds(row, piece.shape[0]), at])
            for piece, row in zip(pieces, firsts)
        ]

    def wait(copies):
        for copy in copies:
            copy.wait()

    def block(i):
        return w_s[:, i * BLOCK : (i + 1) * BLOCK]

    x_in = [fetch(rows_hbm.at[:, pl.ds(0, cap), :], x_s)]
    y_in = [fetch(rows_hbm.at[:, pl.ds(cap, cap), :], y_s)]
    y_in += fetch_blocks(0, 1)
    u_in = fetch_blocks(1, 3)
    wait(x_in)
    zero = jnp.zeros((rank, BLOCK), BF16)
    for step in range(steps):
        at = slice(step * BLOCK, (step + 1) * BLOCK)
        win = (0.5 * win_s[:, at].astype(F32)).astype(BF16)
        dnt = (0.5 * dnt_s[:, at].astype(F32)).astype(BF16)
        extra = [[win[:rank], zero], [zero, win[rank:]], [dnt, zero]]
        for part in range(3):
            i = 3 * step + part
            w_s[width:, i * BLOCK : (i + 1) * BLOCK] = jnp.concatenate(extra[part], axis=0)
    x_rows[:, :width] = x_s[...].reshape(slots, width)
    low = dot_nn(x_rows[:, :width], narrow_s[...])
    low_t = low.T.astype(BF16)
    x_rows[:, width:] = low.astype(BF16)
    rest = fetch_blocks(3, 6)
    wait(y_in)
    y_rows[:, :width] = y_s[...].reshape(slots, width)
    z = dot_nt(y_rows[:, :width], dw_s[...])
    z_t = z.T.astype(BF16)
    z = z.astype(BF16)
    y_rows[:, width:] = jnp.concatenate([z, jnp.zeros_like(z)], axis=1)
    vals = [dot_nn(x_rows[...], block(0))]
    wait(u_in)
    vals += [dot_nn(x_rows[...], block(1)), dot_nn(y_rows[...], block(2))]
    wait(rest)
    for i in range(3, 6):
        vals.append(dot_nn(y_rows[...] if i % 3 == 2 else x_rows[...], block(i)))
    for step in range(steps):
        at = pl.ds(step * BLOCK, BLOCK)
        gate, up, dhid = vals[3 * step : 3 * step + 3]
        sig = jax.nn.sigmoid(gate)
        silu = gate * sig
        hid_s[:, at] = (silu * up).astype(BF16)
        dgate_s[:, at] = (dhid * up * sig * (1.0 + gate * (1.0 - sig))).astype(BF16)
        dup_s[:, at] = (dhid * silu).astype(BF16)

    hlow_t = dot_nt(dnt_s[...], hid_s[...]).astype(BF16)
    vlow_t = jnp.concatenate(
        [dot_nt(win_s[:rank, :], dgate_s[...]), dot_nt(win_s[rank:, :], dup_s[...])], axis=0
    ).astype(BF16)
    dna_s[...] = dot_nn(z_t, hid_s[...])
    inb_s[:rank, :] = dot_nn(low_t[:rank, :], dgate_s[...])
    inb_s[rank:, :] = dot_nn(low_t[rank:, :], dup_s[...])
    dnb_s[...] = dot_nn(hlow_t, y_rows[:, :width])
    ina_s[...] = dot_nn(vlow_t, x_rows[:, :width])

    even = place_ref[1] == 0
    reach = width // 2
    half = rank // 2
    left = lax.broadcasted_iota(jnp.int32, (half, LANES), 1) < LANES // 2
    upper = lax.broadcasted_iota(jnp.int32, (8, LANES), 0) < 4
    for t in range(keep_ref.shape[0]):
        d = dna_s[:, t * LANES : (t + 1) * LANES]
        top, bottom = d[:half], d[half:]
        middle = (
            jnp.where(left, top, pltpu.roll(bottom, LANES // 2, 1)),
            jnp.where(left, pltpu.roll(top, LANES // 2, 1), bottom),
        )
        last = ([], [])
        for b in range(reach // LANES):
            p = dnb_s[8 * t : 8 * t + 8, b * LANES : (b + 1) * LANES]
            q = dnb_s[8 * t : 8 * t + 8, reach + b * LANES : reach + (b + 1) * LANES]
            last[0].append(jnp.where(upper, p, pltpu.roll(q, 4, 0)))
            last[1].append(jnp.where(upper, pltpu.roll(p, 4, 0), q))
        both = []
        for c in range(2):
            j = 2 * t + c
            lines = [ina_s[:, j * LANES : (j + 1) * LANES]]
            for b in range(units // LANES):
                lines.append(inb_s[8 * j : 8 * j + 8, b * LANES : (b + 1) * LANES])
            both.append(jnp.concatenate(lines + [middle[c]] + last[c], axis=0))
        keep_ref[t] = jnp.where(even, both[0], both[1]).astype(BF16)
        send_ref[t] = jnp.where(even, both[1], both[0]).astype(BF16)


def gradients(place, rows, pieces, narrow, win, dnt, dw, parts):
    sources, pair, width = rows.shape
    cap = pair // 2
    slots = sources * cap
    rank, units = dnt.shape
    lines = (2 * rank * units + units * rank + rank * width) // (parts * LANES) + width // parts
    out = pltpu.VMEM((parts // 2, lines, LANES), BF16)
    out_spec = pl.BlockSpec(memory_space=pltpu.VMEM)
    acts = pltpu.VMEM((sources, cap, width), BF16)
    deep = pltpu.VMEM((slots, width + 2 * rank), BF16)
    hidden = pltpu.VMEM((slots, units), BF16)
    return pl.pallas_call(
        functools.partial(gradients_kernel, parts // 2),
        in_specs=[pl.BlockSpec(memory_space=pltpu.SMEM)]
        + [pl.BlockSpec(memory_space=pl.ANY)]
        + [pl.BlockSpec(memory_space=pltpu.VMEM)] * 4
        + [pl.BlockSpec(memory_space=pl.ANY)] * len(pieces),
        out_shape=(out, out),
        out_specs=(out_spec, out_spec),
        scratch_shapes=[
            deep,
            deep,
            acts,
            acts,
            pltpu.VMEM((width + 2 * rank, 3 * units), BF16),
            hidden,
            hidden,
            hidden,
            pltpu.VMEM((2 * rank, units), F32),
            pltpu.VMEM((rank, units), F32),
            pltpu.VMEM((rank, width), F32),
            pltpu.VMEM((2 * rank, width), F32),
            pltpu.SemaphoreType.DMA((6 + 3 * len(pieces) * (units // BLOCK),)),
        ],
        cost_estimate=pl.CostEstimate(
            flops=2 * slots * width * (3 * units + 6 * rank),
            bytes_accessed=2 * width * (2 * slots + 3 * units),
            transcendentals=slots * units,
        ),
        compiler_params=pltpu.CompilerParams(vmem_limit_bytes=VMEM),
        name="gradients",
    )(place, *in_hbm(rows), *in_vmem(narrow, dw, dnt, win), *in_hbm(*pieces))


def finish_kernel(factor, parts_ref, ina_ref, inb_ref, dna_ref, dnb_ref):
    total = parts_ref[0].astype(F32)
    for i in range(1, parts_ref.shape[0]):
        total += parts_ref[i].astype(F32)
    total *= factor
    width = ina_ref.shape[1]
    ina_ref[0] = total[:width].T
    at = width
    for b in range(inb_ref.shape[2] // LANES):
        inb_ref[0, :, b * LANES : (b + 1) * LANES] = total[at : at + 8]
        at += 8
    half = dna_ref.shape[2] // 2
    d = total[at : at + half]
    at += half
    both = jnp.concatenate([d, pltpu.roll(d, LANES // 2, 1)], axis=0)
    dna_ref[0] = both.T[: dna_ref.shape[1]]
    reach = dnb_ref.shape[2] // 2
    for b in range(reach // LANES):
        e = total[at : at + 8]
        at += 8
        dnb_ref[0, :, b * LANES : (b + 1) * LANES] = e[:4]
        dnb_ref[0, :, reach + b * LANES : reach + (b + 1) * LANES] = e[4:]


def finish(parts, factor, shapes):
    return pl.pallas_call(
        functools.partial(finish_kernel, factor),
        out_shape=tuple(jax.ShapeDtypeStruct(s, F32) for s in shapes),
        name="sum_parts",
    )(*in_vmem(parts))


def body(
    tokens,
    output_gradient,
    selected_expert_index,
    routing_weight_rows,
    fixed_gate_up_weight,
    fixed_down_weight_flipped,
    gate_up_adapter_narrow,
    gate_up_adapter_widen,
    down_adapter_narrow,
    down_adapter_widen,
):
    experts = lax.axis_size("expert")
    groups = lax.axis_size("dp")
    tok_rows, model_width = tokens.shape
    cap = tok_rows // 8
    width = fixed_down_weight_flipped.shape[2]
    rank = down_adapter_narrow.shape[2]
    factor = 0.5 / math.sqrt(tok_rows * groups * experts)
    pieces = gather_weights(column_blocks(fixed_gate_up_weight[0], fixed_down_weight_flipped[0]))
    rows = pack_rows(
        selected_expert_index.T, routing_weight_rows.T, tokens, output_gradient, experts, cap
    )
    rows = lax.all_to_all(rows, "expert", 0, 0, tiled=True)
    index = lax.axis_index("dp").astype(jnp.int32)
    place = jnp.stack([index // 2, index % 2])
    keep, send = gradients(
        place,
        rows,
        pieces,
        gate_up_adapter_narrow[0],
        gate_up_adapter_widen[0],
        down_adapter_narrow[0].T,
        down_adapter_widen[0],
        groups,
    )
    other = lax.ppermute(send, "dp", [(i, i ^ 1) for i in range(groups)])
    pair = (keep.astype(F32) + other.astype(F32)).astype(BF16)
    lines = [[2 * i + c for i in range(groups // 2)] for c in range(2)]
    parts = lax.all_to_all(pair, "dp", 0, 0, tiled=True, axis_index_groups=lines)
    shapes = (
        (1, model_width // groups, 2 * rank),
        (1, 2 * rank // groups, width),
        (1, width // groups, rank),
        (1, rank // groups, model_width),
    )
    return finish(parts, factor, shapes)


def solution(mesh):
    in_specs = (
        P(("dp", "expert"), None),
        P(("dp", "expert"), None),
        P(("dp", "expert"), None),
        P(("dp", "expert"), None),
        P("expert", "dp", None),
        P("expert", "dp", None),
        P("expert", None, None),
        P("expert", None, None),
        P("expert", None, None),
        P("expert", None, None),
    )
    out_specs = (
        P("expert", "dp", None),
        P("expert", "dp", None),
        P("expert", "dp", None),
        P("expert", "dp", None),
    )
    return jax.shard_map(body, mesh=mesh, in_specs=in_specs, out_specs=out_specs, check_vma=False)
```

```python
import functools
import math

import jax
import jax.numpy as jnp
from jax import lax
from jax.experimental import pallas as pl
from jax.experimental.pallas import tpu as pltpu
from jax.sharding import PartitionSpec as P

F32 = jnp.float32
BF16 = jnp.bfloat16
LANES = 128
BLOCK = 512
VMEM = 44 * 2**20


def in_hbm(*arrays):
    return [pltpu.with_memory_space_constraint(a, pltpu.HBM) for a in arrays]


def in_vmem(*arrays):
    return [pltpu.with_memory_space_constraint(a, pltpu.VMEM) for a in arrays]


def dot_nt(a, b):
    return lax.dot_general(a, b, (((1,), (1,)), ((), ())), preferred_element_type=F32)


def dot_nn(a, b):
    return lax.dot_general(a, b, (((1,), (0,)), ((), ())), preferred_element_type=F32)


def slot_ranks(sel, experts):
    topk, toks = sel.shape
    ids = lax.broadcasted_iota(jnp.int32, (experts, toks), 0)
    chosen = jnp.zeros((experts, toks), F32)
    for k in range(topk):
        chosen += jnp.where(sel[k : k + 1, :] == ids, 1.0, 0.0)
    earlier = lax.broadcasted_iota(jnp.int32, (toks, toks), 0) < lax.broadcasted_iota(
        jnp.int32, (toks, toks), 1
    )
    before = dot_nn(chosen.astype(BF16), jnp.where(earlier, 1.0, 0.0).astype(BF16))
    return jnp.where(chosen > 0.0, before, -1.0)


def pack_kernel(
    cap, sel_hbm, wgt_hbm, tok_hbm, cot_hbm, out_hbm, sel_s, wgt_s, tok_s, cot_s, out_s, hot_s, row_s, sems
):
    experts, _, width = out_s.shape
    cols = width // 8

    def fetch(src, dst, i):
        copy = pltpu.make_async_copy(src, dst, sems.at[i])
        copy.start()
        return copy

    first = [fetch(sel_hbm, sel_s, 0), fetch(wgt_hbm, wgt_s, 1)]
    tok_in = fetch(tok_hbm, tok_s, 2)
    cot_in = fetch(cot_hbm, cot_s, 3)
    for copy in first:
        copy.wait()
    sel = sel_s[...]
    rank = slot_ranks(sel, experts)
    ids = lax.broadcasted_iota(jnp.int32, rank.shape, 0)
    wgt = jnp.zeros(rank.shape, F32)
    for k in range(sel.shape[0]):
        wgt += jnp.where(sel[k : k + 1, :] == ids, wgt_s[k : k + 1, :], 0.0)
    slot = lax.broadcasted_iota(jnp.int32, (cap, rank.shape[1]), 0).astype(F32)
    for e in range(experts):
        taken = rank[e : e + 1, :] == slot
        rows = pl.ds(e * cap, cap)
        hot_s[rows, :] = jnp.where(taken, 1.0, 0.0).astype(BF16)
        weight = jnp.sum(jnp.where(taken, wgt[e : e + 1, :], 0.0), axis=1, keepdims=True)
        row_s[rows, :] = jnp.broadcast_to(weight, (cap, LANES))
    tok_in.wait()
    cot_in.wait()
    copies = []
    for i in range(width // cols):
        at = pl.ds(i * cols, cols)
        x = dot_nn(hot_s[...], tok_s[:, at]).astype(BF16)
        out_s[:, :cap, at] = x.reshape(experts, cap, cols)
        y = dot_nn(hot_s[...], cot_s[:, at])
        y = (jnp.concatenate([row_s[...]] * (cols // LANES), axis=1) * y).astype(BF16)
        out_s[:, cap:, at] = y.reshape(experts, cap, cols)
        copies.append(fetch(out_s.at[:, :, at], out_hbm.at[:, :, at], 4 + i))
    for copy in copies:
        copy.wait()


def pack_rows(sel_t, wgt_t, tok, cot, experts, cap):
    toks, width = tok.shape
    like = lambda a: pltpu.VMEM(a.shape, a.dtype)
    out = pltpu.HBM((experts, 2 * cap, width), BF16)
    return pl.pallas_call(
        functools.partial(pack_kernel, cap),
        in_specs=[pl.BlockSpec(memory_space=pltpu.HBM)] * 4,
        out_shape=out,
        out_specs=pl.BlockSpec(memory_space=pltpu.HBM),
        scratch_shapes=[
            like(sel_t),
            like(wgt_t),
            like(tok),
            like(cot),
            pltpu.VMEM(out.shape, BF16),
            pltpu.VMEM((experts * cap, toks), BF16),
            pltpu.VMEM((experts * cap, LANES), F32),
            pltpu.SemaphoreType.DMA((12,)),
        ],
        cost_estimate=pl.CostEstimate(
            flops=4 * experts * cap * toks * width,
            bytes_accessed=4 * width * (toks + experts * cap),
            transcendentals=0,
        ),
        compiler_params=pltpu.CompilerParams(vmem_limit_bytes=VMEM),
        name="pack_rows",
    )(*in_hbm(sel_t, wgt_t, tok, cot))


def column_blocks(gate_up, down):
    units = down.shape[1]
    cut = lambda a, first: a[:, first : first + BLOCK]
    blocks = []
    for at in range(0, units, BLOCK):
        blocks += [cut(gate_up, at), cut(gate_up, units + at), cut(down, at)]
    return blocks


def gather_weights(shards):
    groups = lax.axis_size("dp")
    chips = groups // 2
    core = lax.axis_index("dp") % 2
    swap = lambda a: lax.ppermute(a, "dp", [(i, i ^ 1) for i in range(groups)])
    ring = lambda a, way: lax.ppermute(a, "dp", [(i, (i + 2 * way(i)) % groups) for i in range(groups)])
    up = down = jnp.concatenate(shards, axis=1)
    held = [up]
    for _ in range(1, chips // 2):
        up = ring(up, lambda i: 1)
        down = ring(down, lambda i: -1)
        held += [up, down]
    held.append(ring(jnp.where(core == 0, up, down), lambda i: 1 if i % 2 == 0 else -1))
    return held + [swap(a) for a in held]


def piece_rows(chips, lines, chip, core):
    starts = [chip]
    for hop in range(1, chips // 2):
        starts += [chip - hop, chip + hop]
    starts.append(chip + chips // 2)
    return [
        pl.multiple_of((2 * lax.rem(at + chips, chips) + part) * lines, lines)
        for part in (core, 1 - core)
        for at in starts
    ]


def first_kernel(chips, place_ref, win_ref, *refs):
    pieces, (out_ref, sems) = refs[: 2 * chips], refs[2 * chips :]
    firsts = piece_rows(chips, pieces[0].shape[0], place_ref[0], place_ref[1])
    copies = []
    for i, (piece, row) in enumerate(zip(pieces, firsts)):
        rows = pl.ds(row, piece.shape[0])
        copies.append(
            pltpu.make_async_copy(piece.at[:, pl.ds(0, BLOCK)], out_ref.at[rows, :], sems.at[i])
        )
        copies[-1].start()
    rank = win_ref.shape[0] // 2
    depth = out_ref.shape[0] - 2 * rank
    win = (0.5 * win_ref[:rank, :BLOCK].astype(F32)).astype(BF16)
    out_ref[depth:, :] = jnp.concatenate([win, jnp.zeros_like(win)], axis=0)
    for copy in copies:
        copy.wait()


def first_block(place, pieces, win):
    whole = pl.BlockSpec(memory_space=pltpu.VMEM)
    rows = len(pieces) * pieces[0].shape[0] + win.shape[0]
    return pl.pallas_call(
        functools.partial(first_kernel, len(pieces) // 2),
        in_specs=[pl.BlockSpec(memory_space=pltpu.SMEM), whole]
        + [pl.BlockSpec(memory_space=pl.ANY)] * len(pieces),
        out_shape=pltpu.VMEM((rows, BLOCK), BF16),
        out_specs=whole,
        scratch_shapes=[pltpu.SemaphoreType.DMA((len(pieces),))],
        cost_estimate=pl.CostEstimate(
            flops=0, bytes_accessed=4 * rows * BLOCK, transcendentals=0
        ),
        compiler_params=pltpu.CompilerParams(vmem_limit_bytes=8 * 2**20),
        name="first_block",
    )(place, *in_vmem(win), *in_hbm(*pieces))


def gradients_kernel(
    chips,
    place_ref,
    rows_hbm,
    dw_hbm,
    narrow_s,
    dnt_s,
    win_s,
    first_ref,
    *refs,
):
    pieces, refs = refs[: 2 * chips], refs[2 * chips :]
    keep_ref, send_ref, x_rows, y_rows, x_s, y_s, dw_s, w_s = refs[:8]
    hid_s, dgate_s, dup_s, inb_s, dna_s, dnb_s, ina_s, sems = refs[8:]
    slots = x_rows.shape[0]
    cap, width = x_s.shape[1:]
    rank, units = dnt_s.shape
    steps = units // BLOCK
    firsts = piece_rows(chips, pieces[0].shape[0], place_ref[0], place_ref[1])
    used = iter(range(sems.shape[0]))

    def fetch(src, dst):
        copy = pltpu.make_async_copy(src, dst, sems.at[next(used)])
        copy.start()
        return copy

    def fetch_blocks(first, last):
        at = pl.ds(first * BLOCK, (last - first) * BLOCK)
        return [
            fetch(piece.at[:, at], w_s.at[pl.ds(row, piece.shape[0]), at])
            for piece, row in zip(pieces, firsts)
        ]

    def wait(copies):
        for copy in copies:
            copy.wait()

    def block(i):
        return w_s[:, i * BLOCK : (i + 1) * BLOCK]

    x_in = [fetch(rows_hbm.at[:, pl.ds(0, cap), :], x_s)]
    y_in = [fetch(rows_hbm.at[:, pl.ds(cap, cap), :], y_s), fetch(dw_hbm, dw_s)]
    y_in += fetch_blocks(1, 3)
    wait(x_in)
    zero = jnp.zeros((rank, BLOCK), BF16)
    for step in range(steps):
        at = slice(step * BLOCK, (step + 1) * BLOCK)
        win = (0.5 * win_s[:, at].astype(F32)).astype(BF16)
        dnt = (0.5 * dnt_s[:, at].astype(F32)).astype(BF16)
        extra = [[win[:rank], zero], [zero, win[rank:]], [dnt, zero]]
        for part in range(3):
            i = 3 * step + part
            w_s[width:, i * BLOCK : (i + 1) * BLOCK] = jnp.concatenate(extra[part], axis=0)
    x_rows[:, :width] = x_s[...].reshape(slots, width)
    low = dot_nn(x_rows[:, :width], narrow_s[...])
    low_t = low.T.astype(BF16)
    x_rows[:, width:] = low.astype(BF16)
    vals = [dot_nn(x_rows[...], first_ref[...])]
    rest = fetch_blocks(3, 6)
    wait(y_in)
    y_rows[:, :width] = y_s[...].reshape(slots, width)
    z = dot_nt(y_rows[:, :width], dw_s[...])
    z_t = z.T.astype(BF16)
    z = z.astype(BF16)
    y_rows[:, width:] = jnp.concatenate([z, jnp.zeros_like(z)], axis=1)
    vals += [dot_nn(x_rows[...], block(1)), dot_nn(y_rows[...], block(2))]
    wait(rest)
    for i in range(3, 6):
        vals.append(dot_nn(y_rows[...] if i % 3 == 2 else x_rows[...], block(i)))
    for step in range(steps):
        at = pl.ds(step * BLOCK, BLOCK)
        gate, up, dhid = vals[3 * step : 3 * step + 3]
        sig = jax.nn.sigmoid(gate)
        silu = gate * sig
        hid_s[:, at] = (silu * up).astype(BF16)
        dgate_s[:, at] = (dhid * up * sig * (1.0 + gate * (1.0 - sig))).astype(BF16)
        dup_s[:, at] = (dhid * silu).astype(BF16)

    hlow_t = dot_nt(dnt_s[...], hid_s[...]).astype(BF16)
    vlow_t = jnp.concatenate(
        [dot_nt(win_s[:rank, :], dgate_s[...]), dot_nt(win_s[rank:, :], dup_s[...])], axis=0
    ).astype(BF16)
    dna_s[...] = dot_nn(z_t, hid_s[...])
    inb_s[:rank, :] = dot_nn(low_t[:rank, :], dgate_s[...])
    inb_s[rank:, :] = dot_nn(low_t[rank:, :], dup_s[...])
    dnb_s[...] = dot_nn(hlow_t, y_rows[:, :width])
    ina_s[...] = dot_nn(vlow_t, x_rows[:, :width])

    even = place_ref[1] == 0
    reach = width // 2
    half = rank // 2
    left = lax.broadcasted_iota(jnp.int32, (half, LANES), 1) < LANES // 2
    upper = lax.broadcasted_iota(jnp.int32, (8, LANES), 0) < 4
    for t in range(keep_ref.shape[0]):
        d = dna_s[:, t * LANES : (t + 1) * LANES]
        top, bottom = d[:half], d[half:]
        middle = (
            jnp.where(left, top, pltpu.roll(bottom, LANES // 2, 1)),
            jnp.where(left, pltpu.roll(top, LANES // 2, 1), bottom),
        )
        last = ([], [])
        for b in range(reach // LANES):
            p = dnb_s[8 * t : 8 * t + 8, b * LANES : (b + 1) * LANES]
            q = dnb_s[8 * t : 8 * t + 8, reach + b * LANES : reach + (b + 1) * LANES]
            last[0].append(jnp.where(upper, p, pltpu.roll(q, 4, 0)))
            last[1].append(jnp.where(upper, pltpu.roll(p, 4, 0), q))
        both = []
        for c in range(2):
            j = 2 * t + c
            lines = [ina_s[:, j * LANES : (j + 1) * LANES]]
            for b in range(units // LANES):
                lines.append(inb_s[8 * j : 8 * j + 8, b * LANES : (b + 1) * LANES])
            both.append(jnp.concatenate(lines + [middle[c]] + last[c], axis=0))
        keep_ref[t] = jnp.where(even, both[0], both[1]).astype(BF16)
        send_ref[t] = jnp.where(even, both[1], both[0]).astype(BF16)


def gradients(place, rows, pieces, narrow, win, dnt, dw, parts):
    sources, pair, width = rows.shape
    cap = pair // 2
    slots = sources * cap
    rank, units = dnt.shape
    lines = (2 * rank * units + units * rank + rank * width) // (parts * LANES) + width // parts
    out = pltpu.VMEM((parts // 2, lines, LANES), BF16)
    out_spec = pl.BlockSpec(memory_space=pltpu.VMEM)
    acts = pltpu.VMEM((sources, cap, width), BF16)
    deep = pltpu.VMEM((slots, width + 2 * rank), BF16)
    hidden = pltpu.VMEM((slots, units), BF16)
    first = first_block(place, pieces, win)
    return pl.pallas_call(
        functools.partial(gradients_kernel, parts // 2),
        in_specs=[pl.BlockSpec(memory_space=pltpu.SMEM)]
        + [pl.BlockSpec(memory_space=pl.ANY)] * 2
        + [pl.BlockSpec(memory_space=pltpu.VMEM)] * 4
        + [pl.BlockSpec(memory_space=pl.ANY)] * len(pieces),
        out_shape=(out, out),
        out_specs=(out_spec, out_spec),
        scratch_shapes=[
            deep,
            deep,
            acts,
            acts,
            pltpu.VMEM(dw.shape, BF16),
            pltpu.VMEM((width + 2 * rank, 3 * units), BF16),
            hidden,
            hidden,
            hidden,
            pltpu.VMEM((2 * rank, units), F32),
            pltpu.VMEM((rank, units), F32),
            pltpu.VMEM((rank, width), F32),
            pltpu.VMEM((2 * rank, width), F32),
            pltpu.SemaphoreType.DMA((6 + 3 * len(pieces) * (units // BLOCK),)),
        ],
        cost_estimate=pl.CostEstimate(
            flops=2 * slots * width * (3 * units + 6 * rank),
            bytes_accessed=2 * width * (2 * slots + 3 * units),
            transcendentals=slots * units,
        ),
        compiler_params=pltpu.CompilerParams(vmem_limit_bytes=VMEM),
        name="gradients",
    )(place, *in_hbm(rows, dw), *in_vmem(narrow, dnt, win, first), *in_hbm(*pieces))


def finish_kernel(factor, parts_ref, ina_ref, inb_ref, dna_ref, dnb_ref):
    total = parts_ref[0].astype(F32)
    for i in range(1, parts_ref.shape[0]):
        total += parts_ref[i].astype(F32)
    total *= factor
    width = ina_ref.shape[1]
    ina_ref[0] = total[:width].T
    at = width
    for b in range(inb_ref.shape[2] // LANES):
        inb_ref[0, :, b * LANES : (b + 1) * LANES] = total[at : at + 8]
        at += 8
    half = dna_ref.shape[2] // 2
    d = total[at : at + half]
    at += half
    both = jnp.concatenate([d, pltpu.roll(d, LANES // 2, 1)], axis=0)
    dna_ref[0] = both.T[: dna_ref.shape[1]]
    reach = dnb_ref.shape[2] // 2
    for b in range(reach // LANES):
        e = total[at : at + 8]
        at += 8
        dnb_ref[0, :, b * LANES : (b + 1) * LANES] = e[:4]
        dnb_ref[0, :, reach + b * LANES : reach + (b + 1) * LANES] = e[4:]


def finish(parts, factor, shapes):
    return pl.pallas_call(
        functools.partial(finish_kernel, factor),
        out_shape=tuple(jax.ShapeDtypeStruct(s, F32) for s in shapes),
        name="sum_parts",
    )(*in_vmem(parts))


def body(
    tokens,
    output_gradient,
    selected_expert_index,
    routing_weight_rows,
    fixed_gate_up_weight,
    fixed_down_weight_flipped,
    gate_up_adapter_narrow,
    gate_up_adapter_widen,
    down_adapter_narrow,
    down_adapter_widen,
):
    experts = lax.axis_size("expert")
    groups = lax.axis_size("dp")
    tok_rows, model_width = tokens.shape
    cap = tok_rows // 8
    width = fixed_down_weight_flipped.shape[2]
    rank = down_adapter_narrow.shape[2]
    factor = 0.5 / math.sqrt(tok_rows * groups * experts)
    pieces = gather_weights(column_blocks(fixed_gate_up_weight[0], fixed_down_weight_flipped[0]))
    rows = pack_rows(
        selected_expert_index.T, routing_weight_rows.T, tokens, output_gradient, experts, cap
    )
    rows = lax.all_to_all(rows, "expert", 0, 0, tiled=True)
    index = lax.axis_index("dp").astype(jnp.int32)
    place = jnp.stack([index // 2, index % 2])
    keep, send = gradients(
        place,
        rows,
        pieces,
        gate_up_adapter_narrow[0],
        gate_up_adapter_widen[0],
        down_adapter_narrow[0].T,
        down_adapter_widen[0],
        groups,
    )
    other = lax.ppermute(send, "dp", [(i, i ^ 1) for i in range(groups)])
    pair = (keep.astype(F32) + other.astype(F32)).astype(BF16)
    lines = [[2 * i + c for i in range(groups // 2)] for c in range(2)]
    parts = lax.all_to_all(pair, "dp", 0, 0, tiled=True, axis_index_groups=lines)
    shapes = (
        (1, model_width // groups, 2 * rank),
        (1, 2 * rank // groups, width),
        (1, width // groups, rank),
        (1, rank // groups, model_width),
    )
    return finish(parts, factor, shapes)


def solution(mesh):
    in_specs = (
        P(("dp", "expert"), None),
        P(("dp", "expert"), None),
        P(("dp", "expert"), None),
        P(("dp", "expert"), None),
        P("expert", "dp", None),
        P("expert", "dp", None),
        P("expert", None, None),
        P("expert", None, None),
        P("expert", None, None),
        P("expert", None, None),
    )
    out_specs = (
        P("expert", "dp", None),
        P("expert", "dp", None),
        P("expert", "dp", None),
        P("expert", "dp", None),
    )
    return jax.shard_map(body, mesh=mesh, in_specs=in_specs, out_specs=out_specs, check_vma=False)
```

```python
import functools
import math

import jax
import jax.numpy as jnp
from jax import lax
from jax.experimental import pallas as pl
from jax.experimental.pallas import tpu as pltpu
from jax.sharding import PartitionSpec as P

F32 = jnp.float32
BF16 = jnp.bfloat16
LANES = 128
BLOCK = 512
VMEM = 44 * 2**20


def in_hbm(*arrays):
    return [pltpu.with_memory_space_constraint(a, pltpu.HBM) for a in arrays]


def in_vmem(*arrays):
    return [pltpu.with_memory_space_constraint(a, pltpu.VMEM) for a in arrays]


def dot_nt(a, b):
    return lax.dot_general(a, b, (((1,), (1,)), ((), ())), preferred_element_type=F32)


def dot_nn(a, b):
    return lax.dot_general(a, b, (((1,), (0,)), ((), ())), preferred_element_type=F32)


def slot_ranks(sel, experts):
    topk, toks = sel.shape
    ids = lax.broadcasted_iota(jnp.int32, (experts, toks), 0)
    chosen = jnp.zeros((experts, toks), F32)
    for k in range(topk):
        chosen += jnp.where(sel[k : k + 1, :] == ids, 1.0, 0.0)
    earlier = lax.broadcasted_iota(jnp.int32, (toks, toks), 0) < lax.broadcasted_iota(
        jnp.int32, (toks, toks), 1
    )
    before = dot_nn(chosen.astype(BF16), jnp.where(earlier, 1.0, 0.0).astype(BF16))
    return jnp.where(chosen > 0.0, before, -1.0)


def pack_kernel(
    cap, sel_hbm, wgt_hbm, tok_hbm, cot_hbm, out_hbm, sel_s, wgt_s, tok_s, cot_s, out_s, hot_s, row_s, sems
):
    experts, _, width = out_s.shape
    cols = width // 8

    def fetch(src, dst, i):
        copy = pltpu.make_async_copy(src, dst, sems.at[i])
        copy.start()
        return copy

    first = [fetch(sel_hbm, sel_s, 0), fetch(wgt_hbm, wgt_s, 1)]
    tok_in = fetch(tok_hbm, tok_s, 2)
    cot_in = fetch(cot_hbm, cot_s, 3)
    for copy in first:
        copy.wait()
    sel = sel_s[...]
    rank = slot_ranks(sel, experts)
    ids = lax.broadcasted_iota(jnp.int32, rank.shape, 0)
    wgt = jnp.zeros(rank.shape, F32)
    for k in range(sel.shape[0]):
        wgt += jnp.where(sel[k : k + 1, :] == ids, wgt_s[k : k + 1, :], 0.0)
    slot = lax.broadcasted_iota(jnp.int32, (cap, rank.shape[1]), 0).astype(F32)
    for e in range(experts):
        taken = rank[e : e + 1, :] == slot
        rows = pl.ds(e * cap, cap)
        hot_s[rows, :] = jnp.where(taken, 1.0, 0.0).astype(BF16)
        weight = jnp.sum(jnp.where(taken, wgt[e : e + 1, :], 0.0), axis=1, keepdims=True)
        row_s[rows, :] = jnp.broadcast_to(weight, (cap, LANES))
    tok_in.wait()
    cot_in.wait()
    copies = []
    for i in range(width // cols):
        at = pl.ds(i * cols, cols)
        x = dot_nn(hot_s[...], tok_s[:, at]).astype(BF16)
        out_s[:, :cap, at] = x.reshape(experts, cap, cols)
        y = dot_nn(hot_s[...], cot_s[:, at])
        y = (jnp.concatenate([row_s[...]] * (cols // LANES), axis=1) * y).astype(BF16)
        out_s[:, cap:, at] = y.reshape(experts, cap, cols)
        copies.append(fetch(out_s.at[:, :, at], out_hbm.at[:, :, at], 4 + i))
    for copy in copies:
        copy.wait()


def pack_rows(sel_t, wgt_t, tok, cot, experts, cap):
    toks, width = tok.shape
    like = lambda a: pltpu.VMEM(a.shape, a.dtype)
    out = pltpu.HBM((experts, 2 * cap, width), BF16)
    return pl.pallas_call(
        functools.partial(pack_kernel, cap),
        in_specs=[pl.BlockSpec(memory_space=pltpu.HBM)] * 4,
        out_shape=out,
        out_specs=pl.BlockSpec(memory_space=pltpu.HBM),
        scratch_shapes=[
            like(sel_t),
            like(wgt_t),
            like(tok),
            like(cot),
            pltpu.VMEM(out.shape, BF16),
            pltpu.VMEM((experts * cap, toks), BF16),
            pltpu.VMEM((experts * cap, LANES), F32),
            pltpu.SemaphoreType.DMA((12,)),
        ],
        cost_estimate=pl.CostEstimate(
            flops=4 * experts * cap * toks * width,
            bytes_accessed=4 * width * (toks + experts * cap),
            transcendentals=0,
        ),
        compiler_params=pltpu.CompilerParams(vmem_limit_bytes=VMEM),
        name="pack_rows",
    )(*in_hbm(sel_t, wgt_t, tok, cot))


def column_blocks(gate_up, down):
    units = down.shape[1]
    cut = lambda a, first: a[:, first : first + BLOCK]
    blocks = []
    for at in range(0, units, BLOCK):
        blocks += [cut(gate_up, at), cut(gate_up, units + at), cut(down, at)]
    return blocks


def gather_weights(shards):
    groups = lax.axis_size("dp")
    chips = groups // 2
    core = lax.axis_index("dp") % 2
    swap = lambda a: lax.ppermute(a, "dp", [(i, i ^ 1) for i in range(groups)])
    ring = lambda a, way: lax.ppermute(a, "dp", [(i, (i + 2 * way(i)) % groups) for i in range(groups)])
    up = down = jnp.concatenate(shards, axis=1)
    held = [up]
    for _ in range(1, chips // 2):
        up = ring(up, lambda i: 1)
        down = ring(down, lambda i: -1)
        held += [up, down]
    held.append(ring(jnp.where(core == 0, up, down), lambda i: 1 if i % 2 == 0 else -1))
    return held + [swap(a) for a in held]


def piece_rows(chips, lines, chip, core):
    starts = [chip]
    for hop in range(1, chips // 2):
        starts += [chip - hop, chip + hop]
    starts.append(chip + chips // 2)
    return [
        pl.multiple_of((2 * lax.rem(at + chips, chips) + part) * lines, lines)
        for part in (core, 1 - core)
        for at in starts
    ]


def first_kernel(chips, place_ref, win_ref, *refs):
    pieces, (out_ref, sems) = refs[: 2 * chips], refs[2 * chips :]
    firsts = piece_rows(chips, pieces[0].shape[0], place_ref[0], place_ref[1])
    copies = []
    for i, (piece, row) in enumerate(zip(pieces, firsts)):
        rows = pl.ds(row, piece.shape[0])
        copies.append(
            pltpu.make_async_copy(piece.at[:, pl.ds(0, BLOCK)], out_ref.at[rows, :], sems.at[i])
        )
        copies[-1].start()
    rank = win_ref.shape[0] // 2
    depth = out_ref.shape[0] - 2 * rank
    win = (0.5 * win_ref[:rank, :BLOCK].astype(F32)).astype(BF16)
    out_ref[depth:, :] = jnp.concatenate([win, jnp.zeros_like(win)], axis=0)
    for copy in copies:
        copy.wait()


def first_block(place, pieces, win):
    whole = pl.BlockSpec(memory_space=pltpu.VMEM)
    rows = len(pieces) * pieces[0].shape[0] + win.shape[0]
    return pl.pallas_call(
        functools.partial(first_kernel, len(pieces) // 2),
        in_specs=[pl.BlockSpec(memory_space=pltpu.SMEM), whole]
        + [pl.BlockSpec(memory_space=pl.ANY)] * len(pieces),
        out_shape=pltpu.VMEM((rows, BLOCK), BF16),
        out_specs=whole,
        scratch_shapes=[pltpu.SemaphoreType.DMA((len(pieces),))],
        cost_estimate=pl.CostEstimate(
            flops=0, bytes_accessed=4 * rows * BLOCK, transcendentals=0
        ),
        compiler_params=pltpu.CompilerParams(vmem_limit_bytes=8 * 2**20),
        name="first_block",
    )(place, *in_vmem(win), *in_hbm(*pieces))


def gradients_kernel(
    chips,
    place_ref,
    rows_hbm,
    dw_hbm,
    narrow_s,
    dnt_s,
    win_s,
    first_ref,
    *refs,
):
    pieces, refs = refs[: 2 * chips], refs[2 * chips :]
    keep_ref, send_ref, x_rows, y_rows, x_s, y_s, dw_s, w_s = refs[:8]
    hid_s, dgate_s, dup_s, inb_s, dna_s, dnb_s, ina_s, sems = refs[8:]
    slots = x_rows.shape[0]
    cap, width = x_s.shape[1:]
    rank, units = dnt_s.shape
    steps = units // BLOCK
    firsts = piece_rows(chips, pieces[0].shape[0], place_ref[0], place_ref[1])
    used = iter(range(sems.shape[0]))

    def fetch(src, dst):
        copy = pltpu.make_async_copy(src, dst, sems.at[next(used)])
        copy.start()
        return copy

    def fetch_blocks(first, last):
        at = pl.ds(first * BLOCK, (last - first) * BLOCK)
        return [
            fetch(piece.at[:, at], w_s.at[pl.ds(row, piece.shape[0]), at])
            for piece, row in zip(pieces, firsts)
        ]

    def wait(copies):
        for copy in copies:
            copy.wait()

    def block(i):
        return w_s[:, i * BLOCK : (i + 1) * BLOCK]

    x_in = [fetch(rows_hbm.at[:, pl.ds(0, cap), :], x_s)]
    y_in = [fetch(rows_hbm.at[:, pl.ds(cap, cap), :], y_s), fetch(dw_hbm, dw_s)]
    y_in += fetch_blocks(1, 3)
    wait(x_in)
    zero = jnp.zeros((rank, BLOCK), BF16)
    for step in range(steps):
        at = slice(step * BLOCK, (step + 1) * BLOCK)
        win = (0.5 * win_s[:, at].astype(F32)).astype(BF16)
        dnt = (0.5 * dnt_s[:, at].astype(F32)).astype(BF16)
        extra = [[win[:rank], zero], [zero, win[rank:]], [dnt, zero]]
        for part in range(3):
            i = 3 * step + part
            w_s[width:, i * BLOCK : (i + 1) * BLOCK] = jnp.concatenate(extra[part], axis=0)
    x_rows[:, :width] = x_s[...].reshape(slots, width)
    low_t = dot_nt(narrow_s[...], x_rows[:, :width])
    x_rows[:, width:] = low_t.T.astype(BF16)
    low_t = low_t.astype(BF16)
    vals = [dot_nn(x_rows[...], first_ref[...])]
    rest = fetch_blocks(3, 6)
    wait(y_in)
    y_rows[:, :width] = y_s[...].reshape(slots, width)
    z_t = dot_nt(dw_s[...], y_rows[:, :width])
    z = z_t.T.astype(BF16)
    z_t = z_t.astype(BF16)
    y_rows[:, width:] = jnp.concatenate([z, jnp.zeros_like(z)], axis=1)
    vals += [dot_nn(x_rows[...], block(1)), dot_nn(y_rows[...], block(2))]
    wait(rest)
    for i in range(3, 6):
        vals.append(dot_nn(y_rows[...] if i % 3 == 2 else x_rows[...], block(i)))
    for step in range(steps):
        at = pl.ds(step * BLOCK, BLOCK)
        gate, up, dhid = vals[3 * step : 3 * step + 3]
        sig = jax.nn.sigmoid(gate)
        silu = gate * sig
        hid_s[:, at] = (silu * up).astype(BF16)
        dgate_s[:, at] = (dhid * up * sig * (1.0 + gate * (1.0 - sig))).astype(BF16)
        dup_s[:, at] = (dhid * silu).astype(BF16)

    hlow_t = dot_nt(dnt_s[...], hid_s[...]).astype(BF16)
    vlow_t = jnp.concatenate(
        [dot_nt(win_s[:rank, :], dgate_s[...]), dot_nt(win_s[rank:, :], dup_s[...])], axis=0
    ).astype(BF16)
    dna_s[...] = dot_nn(z_t, hid_s[...])
    inb_s[:rank, :] = dot_nn(low_t[:rank, :], dgate_s[...])
    inb_s[rank:, :] = dot_nn(low_t[rank:, :], dup_s[...])
    dnb_s[...] = dot_nn(hlow_t, y_rows[:, :width])
    ina_s[...] = dot_nn(vlow_t, x_rows[:, :width])

    even = place_ref[1] == 0
    reach = width // 2
    half = rank // 2
    left = lax.broadcasted_iota(jnp.int32, (half, LANES), 1) < LANES // 2
    upper = lax.broadcasted_iota(jnp.int32, (8, LANES), 0) < 4
    for t in range(keep_ref.shape[0]):
        d = dna_s[:, t * LANES : (t + 1) * LANES]
        top, bottom = d[:half], d[half:]
        middle = (
            jnp.where(left, top, pltpu.roll(bottom, LANES // 2, 1)),
            jnp.where(left, pltpu.roll(top, LANES // 2, 1), bottom),
        )
        last = ([], [])
        for b in range(reach // LANES):
            p = dnb_s[8 * t : 8 * t + 8, b * LANES : (b + 1) * LANES]
            q = dnb_s[8 * t : 8 * t + 8, reach + b * LANES : reach + (b + 1) * LANES]
            last[0].append(jnp.where(upper, p, pltpu.roll(q, 4, 0)))
            last[1].append(jnp.where(upper, pltpu.roll(p, 4, 0), q))
        both = []
        for c in range(2):
            j = 2 * t + c
            lines = [ina_s[:, j * LANES : (j + 1) * LANES]]
            for b in range(units // LANES):
                lines.append(inb_s[8 * j : 8 * j + 8, b * LANES : (b + 1) * LANES])
            both.append(jnp.concatenate(lines + [middle[c]] + last[c], axis=0))
        keep_ref[t] = jnp.where(even, both[0], both[1]).astype(BF16)
        send_ref[t] = jnp.where(even, both[1], both[0]).astype(BF16)


def gradients(place, rows, pieces, narrow, win, dnt, dw, parts):
    sources, pair, width = rows.shape
    cap = pair // 2
    slots = sources * cap
    rank, units = dnt.shape
    lines = (2 * rank * units + units * rank + rank * width) // (parts * LANES) + width // parts
    out = pltpu.VMEM((parts // 2, lines, LANES), BF16)
    out_spec = pl.BlockSpec(memory_space=pltpu.VMEM)
    acts = pltpu.VMEM((sources, cap, width), BF16)
    deep = pltpu.VMEM((slots, width + 2 * rank), BF16)
    hidden = pltpu.VMEM((slots, units), BF16)
    first = first_block(place, pieces, win)
    return pl.pallas_call(
        functools.partial(gradients_kernel, parts // 2),
        in_specs=[pl.BlockSpec(memory_space=pltpu.SMEM)]
        + [pl.BlockSpec(memory_space=pl.ANY)] * 2
        + [pl.BlockSpec(memory_space=pltpu.VMEM)] * 4
        + [pl.BlockSpec(memory_space=pl.ANY)] * len(pieces),
        out_shape=(out, out),
        out_specs=(out_spec, out_spec),
        scratch_shapes=[
            deep,
            deep,
            acts,
            acts,
            pltpu.VMEM(dw.shape, BF16),
            pltpu.VMEM((width + 2 * rank, 3 * units), BF16),
            hidden,
            hidden,
            hidden,
            pltpu.VMEM((2 * rank, units), F32),
            pltpu.VMEM((rank, units), F32),
            pltpu.VMEM((rank, width), F32),
            pltpu.VMEM((2 * rank, width), F32),
            pltpu.SemaphoreType.DMA((6 + 3 * len(pieces) * (units // BLOCK),)),
        ],
        cost_estimate=pl.CostEstimate(
            flops=2 * slots * width * (3 * units + 6 * rank),
            bytes_accessed=2 * width * (2 * slots + 3 * units),
            transcendentals=slots * units,
        ),
        compiler_params=pltpu.CompilerParams(vmem_limit_bytes=VMEM),
        name="gradients",
    )(place, *in_hbm(rows, dw), *in_vmem(narrow.T, dnt, win, first), *in_hbm(*pieces))


def finish_kernel(factor, parts_ref, ina_ref, inb_ref, dna_ref, dnb_ref):
    total = parts_ref[0].astype(F32)
    for i in range(1, parts_ref.shape[0]):
        total += parts_ref[i].astype(F32)
    total *= factor
    width = ina_ref.shape[1]
    ina_ref[0] = total[:width].T
    at = width
    for b in range(inb_ref.shape[2] // LANES):
        inb_ref[0, :, b * LANES : (b + 1) * LANES] = total[at : at + 8]
        at += 8
    half = dna_ref.shape[2] // 2
    d = total[at : at + half]
    at += half
    both = jnp.concatenate([d, pltpu.roll(d, LANES // 2, 1)], axis=0)
    dna_ref[0] = both.T[: dna_ref.shape[1]]
    reach = dnb_ref.shape[2] // 2
    for b in range(reach // LANES):
        e = total[at : at + 8]
        at += 8
        dnb_ref[0, :, b * LANES : (b + 1) * LANES] = e[:4]
        dnb_ref[0, :, reach + b * LANES : reach + (b + 1) * LANES] = e[4:]


def finish(parts, factor, shapes):
    return pl.pallas_call(
        functools.partial(finish_kernel, factor),
        out_shape=tuple(jax.ShapeDtypeStruct(s, F32) for s in shapes),
        name="sum_parts",
    )(*in_vmem(parts))


def body(
    tokens,
    output_gradient,
    selected_expert_index,
    routing_weight_rows,
    fixed_gate_up_weight,
    fixed_down_weight_flipped,
    gate_up_adapter_narrow,
    gate_up_adapter_widen,
    down_adapter_narrow,
    down_adapter_widen,
):
    experts = lax.axis_size("expert")
    groups = lax.axis_size("dp")
    tok_rows, model_width = tokens.shape
    cap = tok_rows // 8
    width = fixed_down_weight_flipped.shape[2]
    rank = down_adapter_narrow.shape[2]
    factor = 0.5 / math.sqrt(tok_rows * groups * experts)
    pieces = gather_weights(column_blocks(fixed_gate_up_weight[0], fixed_down_weight_flipped[0]))
    rows = pack_rows(
        selected_expert_index.T, routing_weight_rows.T, tokens, output_gradient, experts, cap
    )
    rows = lax.all_to_all(rows, "expert", 0, 0, tiled=True)
    index = lax.axis_index("dp").astype(jnp.int32)
    place = jnp.stack([index // 2, index % 2])
    keep, send = gradients(
        place,
        rows,
        pieces,
        gate_up_adapter_narrow[0],
        gate_up_adapter_widen[0],
        down_adapter_narrow[0].T,
        down_adapter_widen[0],
        groups,
    )
    other = lax.ppermute(send, "dp", [(i, i ^ 1) for i in range(groups)])
    pair = (keep.astype(F32) + other.astype(F32)).astype(BF16)
    lines = [[2 * i + c for i in range(groups // 2)] for c in range(2)]
    parts = lax.all_to_all(pair, "dp", 0, 0, tiled=True, axis_index_groups=lines)
    shapes = (
        (1, model_width // groups, 2 * rank),
        (1, 2 * rank // groups, width),
        (1, width // groups, rank),
        (1, rank // groups, model_width),
    )
    return finish(parts, factor, shapes)


def solution(mesh):
    in_specs = (
        P(("dp", "expert"), None),
        P(("dp", "expert"), None),
        P(("dp", "expert"), None),
        P(("dp", "expert"), None),
        P("expert", "dp", None),
        P("expert", "dp", None),
        P("expert", None, None),
        P("expert", None, None),
        P("expert", None, None),
        P("expert", None, None),
    )
    out_specs = (
        P("expert", "dp", None),
        P("expert", "dp", None),
        P("expert", "dp", None),
        P("expert", "dp", None),
    )
    return jax.shard_map(body, mesh=mesh, in_specs=in_specs, out_specs=out_specs, check_vma=False)
```

```python
import functools
import math

import jax
import jax.numpy as jnp
from jax import lax
from jax.experimental import pallas as pl
from jax.experimental.pallas import tpu as pltpu
from jax.sharding import PartitionSpec as P

F32 = jnp.float32
BF16 = jnp.bfloat16
LANES = 128
BLOCK = 512
VMEM = 44 * 2**20


def in_hbm(*arrays):
    return [pltpu.with_memory_space_constraint(a, pltpu.HBM) for a in arrays]


def in_vmem(*arrays):
    return [pltpu.with_memory_space_constraint(a, pltpu.VMEM) for a in arrays]


def dot_nt(a, b):
    return lax.dot_general(a, b, (((1,), (1,)), ((), ())), preferred_element_type=F32)


def dot_nn(a, b):
    return lax.dot_general(a, b, (((1,), (0,)), ((), ())), preferred_element_type=F32)


def slot_ranks(sel, experts):
    topk, toks = sel.shape
    ids = lax.broadcasted_iota(jnp.int32, (experts, toks), 0)
    chosen = jnp.zeros((experts, toks), F32)
    for k in range(topk):
        chosen += jnp.where(sel[k : k + 1, :] == ids, 1.0, 0.0)
    earlier = lax.broadcasted_iota(jnp.int32, (toks, toks), 0) < lax.broadcasted_iota(
        jnp.int32, (toks, toks), 1
    )
    before = dot_nn(chosen.astype(BF16), jnp.where(earlier, 1.0, 0.0).astype(BF16))
    return jnp.where(chosen > 0.0, before, -1.0)


def pack_kernel(
    cap, sel_hbm, wgt_hbm, tok_hbm, cot_hbm, out_hbm, sel_s, wgt_s, tok_s, cot_s, out_s, hot_s, row_s, sems
):
    experts, _, width = out_s.shape
    cols = width // 8

    def fetch(src, dst, i):
        copy = pltpu.make_async_copy(src, dst, sems.at[i])
        copy.start()
        return copy

    first = [fetch(sel_hbm, sel_s, 0), fetch(wgt_hbm, wgt_s, 1)]
    tok_in = fetch(tok_hbm, tok_s, 2)
    cot_in = fetch(cot_hbm, cot_s, 3)
    for copy in first:
        copy.wait()
    sel = sel_s[...]
    rank = slot_ranks(sel, experts)
    ids = lax.broadcasted_iota(jnp.int32, rank.shape, 0)
    wgt = jnp.zeros(rank.shape, F32)
    for k in range(sel.shape[0]):
        wgt += jnp.where(sel[k : k + 1, :] == ids, wgt_s[k : k + 1, :], 0.0)
    slot = lax.broadcasted_iota(jnp.int32, (cap, rank.shape[1]), 0).astype(F32)
    for e in range(experts):
        taken = rank[e : e + 1, :] == slot
        rows = pl.ds(e * cap, cap)
        hot_s[rows, :] = jnp.where(taken, 1.0, 0.0).astype(BF16)
        weight = jnp.sum(jnp.where(taken, wgt[e : e + 1, :], 0.0), axis=1, keepdims=True)
        row_s[rows, :] = jnp.broadcast_to(weight, (cap, LANES))
    tok_in.wait()
    cot_in.wait()
    copies = []
    for i in range(width // cols):
        at = pl.ds(i * cols, cols)
        x = dot_nn(hot_s[...], tok_s[:, at]).astype(BF16)
        out_s[:, :cap, at] = x.reshape(experts, cap, cols)
        y = dot_nn(hot_s[...], cot_s[:, at])
        y = (jnp.concatenate([row_s[...]] * (cols // LANES), axis=1) * y).astype(BF16)
        out_s[:, cap:, at] = y.reshape(experts, cap, cols)
        copies.append(fetch(out_s.at[:, :, at], out_hbm.at[:, :, at], 4 + i))
    for copy in copies:
        copy.wait()


def pack_rows(sel_t, wgt_t, tok, cot, experts, cap):
    toks, width = tok.shape
    like = lambda a: pltpu.VMEM(a.shape, a.dtype)
    out = pltpu.HBM((experts, 2 * cap, width), BF16)
    return pl.pallas_call(
        functools.partial(pack_kernel, cap),
        in_specs=[pl.BlockSpec(memory_space=pltpu.HBM)] * 4,
        out_shape=out,
        out_specs=pl.BlockSpec(memory_space=pltpu.HBM),
        scratch_shapes=[
            like(sel_t),
            like(wgt_t),
            like(tok),
            like(cot),
            pltpu.VMEM(out.shape, BF16),
            pltpu.VMEM((experts * cap, toks), BF16),
            pltpu.VMEM((experts * cap, LANES), F32),
            pltpu.SemaphoreType.DMA((12,)),
        ],
        cost_estimate=pl.CostEstimate(
            flops=4 * experts * cap * toks * width,
            bytes_accessed=4 * width * (toks + experts * cap),
            transcendentals=0,
        ),
        compiler_params=pltpu.CompilerParams(vmem_limit_bytes=VMEM),
        name="pack_rows",
    )(*in_hbm(sel_t, wgt_t, tok, cot))


def column_blocks(gate_up, down):
    units = down.shape[1]
    cut = lambda a, first: a[:, first : first + BLOCK]
    blocks = []
    for at in range(0, units, BLOCK):
        blocks += [cut(gate_up, at), cut(gate_up, units + at), cut(down, at)]
    return blocks


def gather_weights(shards):
    groups = lax.axis_size("dp")
    chips = groups // 2
    core = lax.axis_index("dp") % 2
    swap = lambda a: lax.ppermute(a, "dp", [(i, i ^ 1) for i in range(groups)])
    ring = lambda a, way: lax.ppermute(a, "dp", [(i, (i + 2 * way(i)) % groups) for i in range(groups)])
    up = down = jnp.concatenate(shards, axis=1)
    held = [up]
    for _ in range(1, chips // 2):
        up = ring(up, lambda i: 1)
        down = ring(down, lambda i: -1)
        held += [up, down]
    held.append(ring(jnp.where(core == 0, up, down), lambda i: 1 if i % 2 == 0 else -1))
    return held + [swap(a) for a in held]


def piece_rows(chips, lines, chip, core):
    starts = [chip]
    for hop in range(1, chips // 2):
        starts += [chip - hop, chip + hop]
    starts.append(chip + chips // 2)
    return [
        pl.multiple_of((2 * lax.rem(at + chips, chips) + part) * lines, lines)
        for part in (core, 1 - core)
        for at in starts
    ]


def first_kernel(chips, place_ref, win_ref, *refs):
    pieces, (out_ref, sems) = refs[: 2 * chips], refs[2 * chips :]
    firsts = piece_rows(chips, pieces[0].shape[0], place_ref[0], place_ref[1])
    copies = []
    for i, (piece, row) in enumerate(zip(pieces, firsts)):
        rows = pl.ds(row, piece.shape[0])
        copies.append(
            pltpu.make_async_copy(piece.at[:, pl.ds(0, BLOCK)], out_ref.at[rows, :], sems.at[i])
        )
        copies[-1].start()
    rank = win_ref.shape[0] // 2
    depth = out_ref.shape[0] - 2 * rank
    win = (0.5 * win_ref[:rank, :BLOCK].astype(F32)).astype(BF16)
    out_ref[depth:, :] = jnp.concatenate([win, jnp.zeros_like(win)], axis=0)
    for copy in copies:
        copy.wait()


def first_block(place, pieces, win):
    whole = pl.BlockSpec(memory_space=pltpu.VMEM)
    rows = len(pieces) * pieces[0].shape[0] + win.shape[0]
    return pl.pallas_call(
        functools.partial(first_kernel, len(pieces) // 2),
        in_specs=[pl.BlockSpec(memory_space=pltpu.SMEM), whole]
        + [pl.BlockSpec(memory_space=pl.ANY)] * len(pieces),
        out_shape=pltpu.VMEM((rows, BLOCK), BF16),
        out_specs=whole,
        scratch_shapes=[pltpu.SemaphoreType.DMA((len(pieces),))],
        cost_estimate=pl.CostEstimate(
            flops=0, bytes_accessed=4 * rows * BLOCK, transcendentals=0
        ),
        compiler_params=pltpu.CompilerParams(vmem_limit_bytes=8 * 2**20),
        name="first_block",
    )(place, *in_vmem(win), *in_hbm(*pieces))


def gradients_kernel(
    chips,
    place_ref,
    rows_hbm,
    dw_hbm,
    narrow_s,
    dnt_s,
    win_s,
    first_ref,
    *refs,
):
    pieces, refs = refs[: 2 * chips], refs[2 * chips :]
    keep_ref, send_ref, x_rows, y_rows, x_s, y_s, dw_s, w_s = refs[:8]
    hid_s, dgate_s, dup_s, inb_s, dna_s, dnb_s, ina_s, sems = refs[8:]
    slots = x_rows.shape[0]
    cap, width = x_s.shape[1:]
    rank, units = dnt_s.shape
    steps = units // BLOCK
    firsts = piece_rows(chips, pieces[0].shape[0], place_ref[0], place_ref[1])
    used = iter(range(sems.shape[0]))

    def fetch(src, dst):
        copy = pltpu.make_async_copy(src, dst, sems.at[next(used)])
        copy.start()
        return copy

    def fetch_blocks(first, last):
        at = pl.ds(first * BLOCK, (last - first) * BLOCK)
        return [
            fetch(piece.at[:, at], w_s.at[pl.ds(row, piece.shape[0]), at])
            for piece, row in zip(pieces, firsts)
        ]

    def wait(copies):
        for copy in copies:
            copy.wait()

    def block(i):
        return w_s[:, i * BLOCK : (i + 1) * BLOCK]

    x_in = [fetch(rows_hbm.at[:, pl.ds(0, cap), :], x_s)]
    y_in = [fetch(rows_hbm.at[:, pl.ds(cap, cap), :], y_s), fetch(dw_hbm, dw_s)]
    y_in += fetch_blocks(1, 3)
    wait(x_in)
    zero = jnp.zeros((rank, BLOCK), BF16)
    for step in range(steps):
        at = slice(step * BLOCK, (step + 1) * BLOCK)
        win = (0.5 * win_s[:, at].astype(F32)).astype(BF16)
        dnt = (0.5 * dnt_s[:, at].astype(F32)).astype(BF16)
        extra = [[win[:rank], zero], [zero, win[rank:]], [dnt, zero]]
        for part in range(3):
            i = 3 * step + part
            w_s[width:, i * BLOCK : (i + 1) * BLOCK] = jnp.concatenate(extra[part], axis=0)
    x_rows[:, :width] = x_s[...].reshape(slots, width)
    low_t = dot_nt(narrow_s[...], x_rows[:, :width])
    x_rows[:, width:] = low_t.T.astype(BF16)
    low_t = low_t.astype(BF16)
    vals = [dot_nn(x_rows[...], first_ref[...])]
    rest = fetch_blocks(3, 6)
    wait(y_in)
    vals.append(dot_nn(x_rows[...], block(1)))
    y_rows[:, :width] = y_s[...].reshape(slots, width)
    z_t = dot_nt(dw_s[...], y_rows[:, :width])
    z = z_t.T.astype(BF16)
    z_t = z_t.astype(BF16)
    y_rows[:, width:] = jnp.concatenate([z, jnp.zeros_like(z)], axis=1)
    vals.append(dot_nn(y_rows[...], block(2)))
    wait(rest)
    for i in range(3, 6):
        vals.append(dot_nn(y_rows[...] if i % 3 == 2 else x_rows[...], block(i)))
    for step in range(steps):
        at = pl.ds(step * BLOCK, BLOCK)
        gate, up, dhid = vals[3 * step : 3 * step + 3]
        sig = jax.nn.sigmoid(gate)
        silu = gate * sig
        hid_s[:, at] = (silu * up).astype(BF16)
        dgate_s[:, at] = (dhid * up * sig * (1.0 + gate * (1.0 - sig))).astype(BF16)
        dup_s[:, at] = (dhid * silu).astype(BF16)

    hlow_t = dot_nt(dnt_s[...], hid_s[...]).astype(BF16)
    vlow_t = jnp.concatenate(
        [dot_nt(win_s[:rank, :], dgate_s[...]), dot_nt(win_s[rank:, :], dup_s[...])], axis=0
    ).astype(BF16)
    dna_s[...] = dot_nn(z_t, hid_s[...])
    inb_s[:rank, :] = dot_nn(low_t[:rank, :], dgate_s[...])
    inb_s[rank:, :] = dot_nn(low_t[rank:, :], dup_s[...])
    dnb_s[...] = dot_nn(hlow_t, y_rows[:, :width])
    ina_s[...] = dot_nn(vlow_t, x_rows[:, :width])

    even = place_ref[1] == 0
    reach = width // 2
    half = rank // 2
    left = lax.broadcasted_iota(jnp.int32, (half, LANES), 1) < LANES // 2
    upper = lax.broadcasted_iota(jnp.int32, (8, LANES), 0) < 4
    for t in range(keep_ref.shape[0]):
        d = dna_s[:, t * LANES : (t + 1) * LANES]
        top, bottom = d[:half], d[half:]
        middle = (
            jnp.where(left, top, pltpu.roll(bottom, LANES // 2, 1)),
            jnp.where(left, pltpu.roll(top, LANES // 2, 1), bottom),
        )
        last = ([], [])
        for b in range(reach // LANES):
            p = dnb_s[8 * t : 8 * t + 8, b * LANES : (b + 1) * LANES]
            q = dnb_s[8 * t : 8 * t + 8, reach + b * LANES : reach + (b + 1) * LANES]
            last[0].append(jnp.where(upper, p, pltpu.roll(q, 4, 0)))
            last[1].append(jnp.where(upper, pltpu.roll(p, 4, 0), q))
        both = []
        for c in range(2):
            j = 2 * t + c
            lines = [ina_s[:, j * LANES : (j + 1) * LANES]]
            for b in range(units // LANES):
                lines.append(inb_s[8 * j : 8 * j + 8, b * LANES : (b + 1) * LANES])
            both.append(jnp.concatenate(lines + [middle[c]] + last[c], axis=0))
        keep_ref[t] = jnp.where(even, both[0], both[1]).astype(BF16)
        send_ref[t] = jnp.where(even, both[1], both[0]).astype(BF16)


def gradients(place, rows, pieces, narrow, win, dnt, dw, parts):
    sources, pair, width = rows.shape
    cap = pair // 2
    slots = sources * cap
    rank, units = dnt.shape
    lines = (2 * rank * units + units * rank + rank * width) // (parts * LANES) + width // parts
    out = pltpu.VMEM((parts // 2, lines, LANES), BF16)
    out_spec = pl.BlockSpec(memory_space=pltpu.VMEM)
    acts = pltpu.VMEM((sources, cap, width), BF16)
    deep = pltpu.VMEM((slots, width + 2 * rank), BF16)
    hidden = pltpu.VMEM((slots, units), BF16)
    first = first_block(place, pieces, win)
    return pl.pallas_call(
        functools.partial(gradients_kernel, parts // 2),
        in_specs=[pl.BlockSpec(memory_space=pltpu.SMEM)]
        + [pl.BlockSpec(memory_space=pl.ANY)] * 2
        + [pl.BlockSpec(memory_space=pltpu.VMEM)] * 4
        + [pl.BlockSpec(memory_space=pl.ANY)] * len(pieces),
        out_shape=(out, out),
        out_specs=(out_spec, out_spec),
        scratch_shapes=[
            deep,
            deep,
            acts,
            acts,
            pltpu.VMEM(dw.shape, BF16),
            pltpu.VMEM((width + 2 * rank, 3 * units), BF16),
            hidden,
            hidden,
            hidden,
            pltpu.VMEM((2 * rank, units), F32),
            pltpu.VMEM((rank, units), F32),
            pltpu.VMEM((rank, width), F32),
            pltpu.VMEM((2 * rank, width), F32),
            pltpu.SemaphoreType.DMA((6 + 3 * len(pieces) * (units // BLOCK),)),
        ],
        cost_estimate=pl.CostEstimate(
            flops=2 * slots * width * (3 * units + 6 * rank),
            bytes_accessed=2 * width * (2 * slots + 3 * units),
            transcendentals=slots * units,
        ),
        compiler_params=pltpu.CompilerParams(vmem_limit_bytes=VMEM),
        name="gradients",
    )(place, *in_hbm(rows, dw), *in_vmem(narrow.T, dnt, win, first), *in_hbm(*pieces))


def finish_kernel(factor, parts_ref, ina_ref, inb_ref, dna_ref, dnb_ref):
    total = parts_ref[0].astype(F32)
    for i in range(1, parts_ref.shape[0]):
        total += parts_ref[i].astype(F32)
    total *= factor
    width = ina_ref.shape[1]
    ina_ref[0] = total[:width].T
    at = width
    for b in range(inb_ref.shape[2] // LANES):
        inb_ref[0, :, b * LANES : (b + 1) * LANES] = total[at : at + 8]
        at += 8
    half = dna_ref.shape[2] // 2
    d = total[at : at + half]
    at += half
    both = jnp.concatenate([d, pltpu.roll(d, LANES // 2, 1)], axis=0)
    dna_ref[0] = both.T[: dna_ref.shape[1]]
    reach = dnb_ref.shape[2] // 2
    for b in range(reach // LANES):
        e = total[at : at + 8]
        at += 8
        dnb_ref[0, :, b * LANES : (b + 1) * LANES] = e[:4]
        dnb_ref[0, :, reach + b * LANES : reach + (b + 1) * LANES] = e[4:]


def finish(parts, factor, shapes):
    return pl.pallas_call(
        functools.partial(finish_kernel, factor),
        out_shape=tuple(jax.ShapeDtypeStruct(s, F32) for s in shapes),
        name="sum_parts",
    )(*in_vmem(parts))


def body(
    tokens,
    output_gradient,
    selected_expert_index,
    routing_weight_rows,
    fixed_gate_up_weight,
    fixed_down_weight_flipped,
    gate_up_adapter_narrow,
    gate_up_adapter_widen,
    down_adapter_narrow,
    down_adapter_widen,
):
    experts = lax.axis_size("expert")
    groups = lax.axis_size("dp")
    tok_rows, model_width = tokens.shape
    cap = tok_rows // 8
    width = fixed_down_weight_flipped.shape[2]
    rank = down_adapter_narrow.shape[2]
    factor = 0.5 / math.sqrt(tok_rows * groups * experts)
    pieces = gather_weights(column_blocks(fixed_gate_up_weight[0], fixed_down_weight_flipped[0]))
    rows = pack_rows(
        selected_expert_index.T, routing_weight_rows.T, tokens, output_gradient, experts, cap
    )
    rows = lax.all_to_all(rows, "expert", 0, 0, tiled=True)
    index = lax.axis_index("dp").astype(jnp.int32)
    place = jnp.stack([index // 2, index % 2])
    keep, send = gradients(
        place,
        rows,
        pieces,
        gate_up_adapter_narrow[0],
        gate_up_adapter_widen[0],
        down_adapter_narrow[0].T,
        down_adapter_widen[0],
        groups,
    )
    other = lax.ppermute(send, "dp", [(i, i ^ 1) for i in range(groups)])
    pair = (keep.astype(F32) + other.astype(F32)).astype(BF16)
    lines = [[2 * i + c for i in range(groups // 2)] for c in range(2)]
    parts = lax.all_to_all(pair, "dp", 0, 0, tiled=True, axis_index_groups=lines)
    shapes = (
        (1, model_width // groups, 2 * rank),
        (1, 2 * rank // groups, width),
        (1, width // groups, rank),
        (1, rank // groups, model_width),
    )
    return finish(parts, factor, shapes)


def solution(mesh):
    in_specs = (
        P(("dp", "expert"), None),
        P(("dp", "expert"), None),
        P(("dp", "expert"), None),
        P(("dp", "expert"), None),
        P("expert", "dp", None),
        P("expert", "dp", None),
        P("expert", None, None),
        P("expert", None, None),
        P("expert", None, None),
        P("expert", None, None),
    )
    out_specs = (
        P("expert", "dp", None),
        P("expert", "dp", None),
        P("expert", "dp", None),
        P("expert", "dp", None),
    )
    return jax.shard_map(body, mesh=mesh, in_specs=in_specs, out_specs=out_specs, check_vma=False)
```
